32 devices in a mesh: replica: 8 (over z, y), shard: 4 (over x, core).
Axes of the slice: x: 2, y: 2, z: 4, core: 2. Of those that a mesh axis runs over, the one named last changes fastest.
Arguments:
- features: bfloat16 [2048, 4096], P('replica', 'shard'), may hold values from -6 to 6
- weight: bfloat16 [128, 1024, 128], P('shard'), may hold values from -0.1875 to 0.1875
- rows_index: int32 [128, 8], replicated, may hold values from 0 to 31, as said below
- cotangent: bfloat16 [2048, 16384], P('replica', 'shard'), may hold values from -6 to 6
Outputs:
- activated: bfloat16 [2048, 16384], P('replica', 'shard')
- input_grad: bfloat16 [2048, 4096], P('replica', 'shard')
- weight_grad: float32 [128, 1024, 128], P('shard', 'replica')
The draws below stay inside these ranges and needn't reach their ends.
Inputs may be any that keep to these rules, and one draw needn't show every extreme that they name: `rows_index`: each block column lists 8 different block rows.
All inputs are finite; a program needn't handle non-finite values.
Results may differ from the reference program's by a relative error of at most 0.02.
Values may be sent and summed in bfloat16 or wider, within the bound.
No kernel may reach another device: no remote copies, remote signals or barrier semaphores. Data moves between devices by JAX's collectives and lax.ppermute only.
A program may use at most 128 MiB of HBM per device.

```python
import math
import jax
import jax.numpy as jnp
from jax import lax

D = 4096
FF = 16384
BLK = 128
K = 8
NBR = 32
NCOL = 128
TOKENS = 2048
N_SHARD = 4


def draw_rows_index(key, part):
    keys = jax.random.split(jax.random.fold_in(key, 7), NCOL)

    def pick_rows(one_key):
        return jax.random.permutation(one_key, jnp.arange(NBR, dtype=jnp.int32))[:K]
    return jax.vmap(pick_rows)(keys).astype(jnp.int32)


def steps_of(stream_key, shape, cuts, least, top_value):
    level = 1.0
    for position, parts in cuts:
        heights = jax.random.uniform(jax.random.fold_in(jax.random.fold_in(stream_key, 6), position), (parts,), jnp.float32, least / len(cuts), top_value / len(cuts))
        level = level * jnp.repeat(jnp.exp(heights), shape[position] // parts).reshape((-1,) + (1,) * (len(shape) - 1 - position))
    return level


def normal_values(rng, shape, scale, limit, pieces=(), kind=jnp.bfloat16):
    values = jax.random.normal(rng, shape, jnp.float32) * scale
    if len(pieces) > 0:
        values = steps_of(rng, shape, pieces, -0.22, 0.18) * values
    return jnp.clip(values, min=-limit, max=limit).astype(kind)


def setup_inputs(seed: int = 0) -> dict:
    splits = jax.random.split(jax.random.key(seed), 5)
    return {
        "features": normal_values(splits[0], (TOKENS, D), 1.0, 6.0, ((0, 8), (1, 4))),
        "weight": normal_values(splits[1], (NCOL, K * BLK, BLK), (K * BLK) ** -0.5, 0.1875, ((0, 4),)),
        "rows_index": draw_rows_index(jax.random.fold_in(splits[4], 71), 0),
        "cotangent": normal_values(splits[3], (TOKENS, FF), 1.0, 6.0, ((0, 8), (1, 4))),
    }


def reference(features, weight, rows_index, cotangent):
    groups = NCOL // N_SHARD
    blocks = features.reshape(TOKENS, NBR, BLK).astype(jnp.float32)
    block_weight_tiles = weight.reshape(NCOL, K, BLK, BLK).astype(jnp.float32)
    cot_blocks = cotangent.reshape(TOKENS, NCOL, BLK)
    positions = jnp.arange(NBR, dtype=jnp.int32)

    def per_group(carry, group):
        columns = group * groups + jnp.arange(groups, dtype=jnp.int32)
        chosen = rows_index[columns]
        resident_weights = block_weight_tiles[columns]
        selected_rows = blocks[:, chosen]
        preactivation = jnp.einsum('defv,efvp->dep', selected_rows, resident_weights)
        sig = jax.nn.sigmoid(preactivation)
        activated = (preactivation * sig).astype(jnp.bfloat16)
        slope = cot_blocks[:, columns].astype(jnp.float32) * sig * (1.0 + preactivation * (1.0 - sig))
        output_difference = lax.optimization_barrier(slope.astype(jnp.bfloat16)).astype(jnp.float32)
        gradient_list = jnp.einsum('qlpf,qlx->lpfx', selected_rows, output_difference)
        backward_result = jnp.einsum('iov,omgv->iomg', output_difference, resident_weights)
        onehot = (chosen[:, :, None] == positions[None, None, :]).astype(jnp.float32)
        partial_value = jnp.einsum('tckr,ckb->tbr', backward_result, onehot)
        partial_value = lax.optimization_barrier(partial_value.astype(jnp.bfloat16)).astype(jnp.float32)
        return (carry + partial_value, (activated, gradient_list))
    start = jnp.zeros((TOKENS, NBR, BLK), jnp.float32)
    summed, (acts, gradient_list) = lax.scan(per_group, start, jnp.arange(N_SHARD, dtype=jnp.int32))
    activated = jnp.transpose(acts, (1, 0, 2, 3)).reshape(TOKENS, FF)
    input_grad = summed.reshape(TOKENS, D).astype(jnp.bfloat16)
    weight_grad = gradient_list.reshape(NCOL, K * BLK, BLK) * (1.0 / math.sqrt(TOKENS))
    return (activated, input_grad, weight_grad)
```

```python
import functools
import math

import jax
import jax.numpy as jnp
from jax import lax
from jax.experimental import pallas as pl
from jax.experimental.pallas import tpu as pltpu
from jax.sharding import PartitionSpec as P

F32 = jnp.float32
BF16 = jnp.bfloat16
ANY = pl.BlockSpec(memory_space=pl.ANY)
PARAMS = pltpu.CompilerParams(
    dimension_semantics=("arbitrary",), vmem_limit_bytes=48 * 1024 * 1024
)
STEP = 4


def copy_in(groups, buf, rows, tab, sems):
    copies = [pltpu.make_async_copy(rows, tab, sems.at[0])]
    top = 0
    for group in groups:
        at = 0
        for ref in group:
            height, width = ref.shape
            copies.append(
                pltpu.make_async_copy(
                    ref,
                    buf.at[pl.ds(top, height), pl.ds(at, width)],
                    sems.at[len(copies)],
                )
            )
            at += width
        top += height
    for copy in copies:
        copy.start()
    for copy in copies:
        copy.wait()


class Index:
    def __init__(self, tab, columns, per_column, fold, side):
        shard = lax.axis_index("shard")
        self.base = shard * columns
        self.flip = shard * fold
        self.tab, self.per_column, self.side = tab, per_column, side

    def block(self, col, k):
        return self.tab[(self.base + col) * self.per_column + k] ^ self.flip

    def lanes(self, col, k):
        return pl.ds(pl.multiple_of(self.block(col, k) * self.side, self.side), self.side)

    def gather(self, buf, col, ks):
        return jnp.concatenate([buf[:, self.lanes(col, k)] for k in ks], axis=1)


def staged_blocks(line):
    r = lax.axis_index("replica")
    z, y = r // 2, r % 2
    inner = (z == 1) | (z == 2)
    one, zero = jnp.int32(1), jnp.int32(0)
    order = [
        jnp.where(inner, one, zero),
        jnp.where(inner, zero, one),
        jnp.int32(2),
        jnp.int32(3),
    ]
    return [jnp.where(z >= line // 2, line - 1 - d, d) * 2 + y for d in order]


def direct_blocks(line):
    r = lax.axis_index("replica")
    z, y = r // 2, r % 2
    return [lax.rem(z + n, line) * 2 + y for n in range(line)]


def forward_column(x, w, cot):
    pre = jnp.dot(x, w, preferred_element_type=F32)
    sig = 1.0 / (1.0 + jnp.exp(-pre))
    delta = (cot.astype(F32) * sig * (1.0 + pre * (1.0 - sig))).astype(BF16)
    return pre, sig, delta


def ranges(splits, step):
    out, start = [], 0
    for n in splits:
        out.append((start // step, (start + n) // step - 1))
        start += n
    return out


def held_at(lo, hi):
    return lambda i: jnp.clip(i, lo, hi) - lo


def forward_kernel(nf, first, columns, fold, splits, *refs):
    rows, feats = refs[0], refs[1 : 1 + nf]
    w_ref, cot_ref = refs[1 + nf : 3 + nf]
    buf, tab, sems = refs[-3:]
    delta_refs = refs[-3 - len(splits) : -3]
    act_ref = refs[-4 - len(splits)]
    step, depth, side = w_ref.shape
    per_column = depth // side
    here = pl.program_id(0)

    @pl.when(here == 0)
    def _():
        copy_in([feats], buf, rows, tab, sems)

    index = Index(tab, columns, per_column, fold, side)
    done = []
    for i in range(step):
        x = index.gather(buf, first + here * step + i, range(per_column))
        lanes = slice(i * side, (i + 1) * side)
        pre, sig, delta = forward_column(x, w_ref[i], cot_ref[:, lanes])
        act_ref[:, lanes] = (pre * sig).astype(BF16)
        done.append(delta)
    row = jnp.concatenate(done, axis=1)
    for ref, (lo, hi) in zip(delta_refs, ranges(splits, step)):

        @pl.when((here >= lo) & (here <= hi))
        def _(ref=ref):
            ref[...] = row


def forward(rows, feats, weight, cotangent, fold, act, first, splits, step, after=()):
    tokens, hidden = cotangent.shape
    columns, depth, side = weight.shape
    width = sum(f.shape[1] for f in feats)
    base = first // step
    args = [rows, *feats, weight, cotangent]
    ins = [ANY] * (1 + len(feats)) + [
        pl.BlockSpec((step, depth, side), lambda i: (base + i, 0, 0)),
        pl.BlockSpec((tokens, step * side), lambda i: (0, base + i)),
    ]
    aliases = {}
    if act is not None:
        aliases = {len(args): 0}
        args.append(act)
    args += after
    ins += [ANY] * (len(args) - len(ins))
    outs = [pl.BlockSpec((tokens, step * side), lambda i: (0, base + i))]
    for lo, hi in ranges(splits, step):
        at = held_at(lo, hi)
        outs.append(pl.BlockSpec((tokens, step * side), lambda i, at=at: (0, at(i))))
    return pl.pallas_call(
        functools.partial(forward_kernel, len(feats), first, columns, fold, splits),
        grid=(sum(splits) // step,),
        in_specs=ins,
        out_specs=outs,
        scratch_shapes=[
            pltpu.VMEM((tokens, width), BF16),
            pltpu.SMEM(rows.shape, jnp.int32),
            pltpu.SemaphoreType.DMA((1 + len(feats),)),
        ],
        out_shape=[jax.ShapeDtypeStruct((tokens, hidden), BF16)]
        + [jax.ShapeDtypeStruct((tokens, n * side), BF16) for n in splits],
        input_output_aliases=aliases,
        compiler_params=PARAMS,
        name="forward",
    )(*args)


def block_grads(index, buf, ks, col, delta, scale):
    side = index.side
    x = index.gather(buf, col, ks)
    grad = lax.dot_general(
        x, delta, (((0,), (0,)), ((), ())), preferred_element_type=F32
    )
    return [
        (grad[p * side : (p + 1) * side] * scale).astype(BF16) for p in range(len(ks))
    ]


def grads_kernel(nf, first, columns, fold, scale, line, direct, *refs):
    rows, mine, other = refs[0], refs[1 : 1 + nf], refs[1 + nf : 1 + 2 * nf]
    w_ref, delta_ref, cot_ref = refs[1 + 2 * nf : 4 + 2 * nf]
    buf, tab, sems = refs[-3:]
    sends = refs[-3 - (line - 1 if direct else 1) : -3]
    own_ref = refs[-4 - len(sends)]
    step, depth, side = w_ref.shape
    per_column = depth // side
    tokens = cot_ref.shape[0]
    here = pl.program_id(0)

    @pl.when(here == 0)
    def _():
        copy_in([mine, other], buf, rows, tab, sems)

    index = Index(tab, columns, per_column, fold, side)
    ks = direct_blocks(line) if direct else staged_blocks(line)
    pair = buf.at[pl.ds(tokens, tokens), :]
    done = []
    for i in range(step):
        x = index.gather(pair, first + here * step + i, range(per_column))
        lanes = slice(i * side, (i + 1) * side)
        _, _, delta = forward_column(x, w_ref[i], cot_ref[:, lanes])
        done.append(jnp.concatenate([delta_ref[:, lanes], delta], axis=0))
    for i in range(step):
        blocks = block_grads(index, buf, ks, first + here * step + i, done[i], scale)
        own_ref[i] = blocks[0]
        for p, block in enumerate(blocks[1:]):
            if direct:
                sends[p][i] = block
            else:
                sends[0][p, i] = block


def grads(
    rows, mine, other, weight, delta, cot_other, skip, count, fold, first, line, scale, direct,
    after=(),
):
    tokens = delta.shape[0]
    columns, depth, side = weight.shape
    width = sum(f.shape[1] for f in mine)
    step = math.gcd(first, skip, count, STEP)
    base, skip = first // step, skip // step
    args = [rows, *mine, *other, weight, delta, cot_other, *after]
    ins = [ANY] * (1 + 2 * len(mine)) + [
        pl.BlockSpec((step, depth, side), lambda i: (base + i, 0, 0)),
        pl.BlockSpec((tokens, step * side), lambda i: (0, base + i)),
        pl.BlockSpec((tokens, step * side), lambda i: (0, skip + i)),
    ]
    ins += [ANY] * (len(args) - len(ins))
    one = jax.ShapeDtypeStruct((count, side, side), BF16)
    one_spec = pl.BlockSpec((step, side, side), lambda i: (i, 0, 0))
    if direct:
        sends, send_specs = [one] * (line - 1), [one_spec] * (line - 1)
    else:
        sends = [jax.ShapeDtypeStruct((line - 1, count, side, side), BF16)]
        send_specs = [pl.BlockSpec((line - 1, step, side, side), lambda i: (0, i, 0, 0))]
    return pl.pallas_call(
        functools.partial(grads_kernel, len(mine), first, columns, fold, scale, line, direct),
        grid=(count // step,),
        in_specs=ins,
        out_specs=[one_spec, *send_specs],
        scratch_shapes=[
            pltpu.VMEM((2 * tokens, width), BF16),
            pltpu.SMEM(rows.shape, jnp.int32),
            pltpu.SemaphoreType.DMA((1 + 2 * len(mine),)),
        ],
        out_shape=[one, *sends],
        compiler_params=PARAMS,
        name="grads",
    )(*args)


def dinput_kernel(nd, fold, groups, *refs):
    rows, deltas, w_ref = refs[0], refs[1 : 1 + nd], refs[1 + nd]
    buf, acc, tab, sems = refs[-4:]
    outs = refs[-4 - len(groups) : -4]
    step, depth, side = w_ref.shape
    per_column = depth // side
    here = pl.program_id(0)

    @pl.when(here == 0)
    def _():
        copy_in([deltas], buf, rows, tab, sems)
        acc[...] = jnp.zeros_like(acc)

    index = Index(tab, buf.shape[1] // side, per_column, fold, side)
    for i in range(step):
        col = here * step + i
        d = buf[:, pl.ds(pl.multiple_of(col * side, side), side)]
        g = lax.dot_general(
            d, w_ref[i], (((1,), (1,)), ((), ())), preferred_element_type=F32
        )
        for k in range(per_column):
            acc[index.block(col, k)] += g[:, k * side : (k + 1) * side]

    @pl.when(here == pl.num_programs(0) - 1)
    def _():
        for out, group in zip(outs, groups):
            blocks = out.shape[2] // side
            for n, piece in enumerate(group):
                for b in range(blocks):
                    out[n, :, b * side : (b + 1) * side] = acc[piece * blocks + b].astype(BF16)


def dinput(rows, weight, deltas, fold, groups, width, step, after=()):
    tokens = deltas[0].shape[0]
    columns, depth, side = weight.shape
    pieces = sum(len(g) for g in groups)
    shapes = [(len(g), tokens, width) for g in groups]
    return pl.pallas_call(
        functools.partial(dinput_kernel, len(deltas), fold, groups),
        grid=(columns // step,),
        in_specs=[ANY] * (1 + len(deltas))
        + [pl.BlockSpec((step, depth, side), lambda i: (i, 0, 0))]
        + [ANY] * len(after),
        out_specs=[pl.BlockSpec(s, lambda i: (0, 0, 0)) for s in shapes],
        scratch_shapes=[
            pltpu.VMEM((tokens, columns * side), BF16),
            pltpu.VMEM((pieces * width // side, tokens, side), F32),
            pltpu.SMEM(rows.shape, jnp.int32),
            pltpu.SemaphoreType.DMA((1 + len(deltas),)),
        ],
        out_shape=[jax.ShapeDtypeStruct(s, BF16) for s in shapes],
        compiler_params=PARAMS,
        name="dinput",
    )(rows, *deltas, weight, *after)


def relay_kernel(jobs, *refs):
    outs = refs[-len(jobs) :]
    for n, (a_at, b_at, count) in enumerate(jobs):
        a, b = refs[2 * n], refs[2 * n + 1]
        for i in range(count):
            outs[n][i] = (a[a_at + i].astype(F32) + b[b_at + i].astype(F32)).astype(BF16)


def relay(*jobs, after=()):
    args, ins, outs, shapes, cuts = [], [], [], [], []
    steps = 2
    for a, a_at, b, b_at, count in jobs:
        part = (a.shape[1] // steps,) + a.shape[2:]
        zeros = (0,) * (a.ndim - 2)
        for x in (a, b):
            args.append(x)
            ins.append(pl.BlockSpec(x.shape[:1] + part, lambda i, z=zeros: (0, i) + z))
        outs.append(pl.BlockSpec((count,) + part, lambda i, z=zeros: (0, i) + z))
        shapes.append(jax.ShapeDtypeStruct((count,) + a.shape[1:], BF16))
        cuts.append((a_at, b_at, count))

    def kernel(*refs):
        relay_kernel(cuts, *refs[: len(args)], *refs[len(args) + len(after) :])

    return pl.pallas_call(
        kernel,
        grid=(steps,),
        in_specs=ins + [ANY] * len(after),
        out_specs=outs,
        out_shape=shapes,
        compiler_params=PARAMS,
        name="relay",
    )(*args, *after)


def cut_kernel(splits, x_ref, *refs):
    refs = refs[-len(splits) :]
    here = pl.program_id(0)
    for ref, (lo, hi) in zip(refs, ranges(splits, 1)):

        @pl.when((here >= lo) & (here <= hi))
        def _(ref=ref):
            ref[...] = x_ref[...]


def cut(x, first, splits, width, after=()):
    height = x.shape[0]
    outs = []
    for lo, hi in ranges(splits, 1):
        at = held_at(lo, hi)
        outs.append(pl.BlockSpec((height, width), lambda i, at=at: (0, at(i))))
    return pl.pallas_call(
        functools.partial(cut_kernel, splits),
        grid=(sum(splits),),
        in_specs=[pl.BlockSpec((height, width), lambda i: (0, first + i))] + [ANY] * len(after),
        out_specs=outs,
        out_shape=[jax.ShapeDtypeStruct((height, n * width), x.dtype) for n in splits],
        compiler_params=PARAMS,
        name="cut",
    )(x, *after)


def gate_kernel(*refs):
    del refs


def gate(x, *after):
    return pl.pallas_call(
        gate_kernel,
        in_specs=[ANY] * (1 + len(after)),
        out_specs=ANY,
        out_shape=jax.ShapeDtypeStruct(x.shape, x.dtype),
        input_output_aliases={0: 0},
        name="gate",
    )(x, *after)


def local_line(features, weight, rows_index, cotangent):
    tokens, held = features.shape
    columns, depth, side = weight.shape
    per_column = depth // side
    replicas, shards = lax.axis_size("replica"), lax.axis_size("shard")
    scale = 1.0 / math.sqrt(tokens * replicas)
    rows = rows_index.reshape(-1)
    fold = held // side
    line = replicas // 2

    def permute(axis, links):
        return lambda x: lax.ppermute(x, axis, links)

    def along(steps):
        return permute("replica", [(a * 2 + p, b * 2 + p) for a, b in steps for p in range(2)])

    cores = permute("shard", [(i, i ^ 1) for i in range(shards)])
    chips = permute("shard", [(i, i ^ 2) for i in range(shards)])
    pairs = permute("replica", [(i, i ^ 1) for i in range(replicas)])
    outer_in = along([(0, 1), (3, 2)])
    middle = along([(1, 2), (2, 1)])
    outer_out = along([(1, 0), (2, 3)])
    shifts = [along([(a, (a + n) % line) for a in range(line)]) for n in range(1, line)]

    sizes = [c * columns // 32 for c in (6, 6, 6, 6, 8)]
    firsts = [sum(sizes[:n]) for n in range(len(sizes))]
    parts = [sizes[0], sizes[1] + sizes[2], sizes[3] + sizes[4]]
    places = [(0, 0), (1, 0), (1, sizes[1]), (2, 0), (2, sizes[3])]

    f0 = features
    f2 = chips(f0)
    u0 = pairs(f0)
    unit = math.gcd(*sizes)
    cots = cut(cotangent, 0, [n // unit for n in parts], unit * side)
    c0, c1, c2 = cs = [pairs(x) for x in cots]
    f1 = cores(f0)
    f3 = cores(f2)
    u1 = cores(u0)
    u2 = chips(u0)
    mine = [f0, f1, f2, f3]
    act, delta = forward(
        rows, mine, weight, cotangent, fold, None, 0, (columns,), STEP, (cots[0],)
    )
    u2 = gate(u2, delta, c0)
    u3 = cores(u2)
    other = [u0, u1, u2, u3]

    def chunk(n, direct, *after):
        part, skip = places[n]
        return grads(
            rows, mine, other, weight, delta, cs[part], skip, sizes[n], fold, firsts[n],
            line, scale, direct, after,
        )

    own0, rest0 = chunk(0, False)
    got0 = outer_in(rest0)
    near, away0, away1 = dinput(
        rows, weight, [delta], fold, ((0, 2), (1,), (3,)), held, STEP, (own0,)
    )
    sib0, sib1 = cores(away0), cores(away1)
    own1, rest1 = chunk(1, False, near)
    got1 = outer_in(rest1)
    (far0,) = relay((rest0, 1, got0, 1, 2), after=(own1,))
    across0 = middle(far0)
    own2, rest2 = chunk(2, False, far0)
    got2 = outer_in(rest2)
    far1, home0 = relay((rest1, 1, got1, 1, 2), (rest0, 0, across0, 1, 1), after=(own2,))
    across1 = middle(far1)
    back0 = outer_out(home0)
    own3, rest3 = chunk(3, False, far1)
    got3 = outer_in(rest3)
    (xsum,) = relay((near, 1, sib1, 0, 1), after=(own3,))
    xback = chips(xsum)
    own4, *sends = chunk(4, True, xsum)
    arrived = [shift(x) for shift, x in zip(shifts, sends)]
    far2, home1 = relay((rest2, 1, got2, 1, 2), (rest1, 0, across1, 1, 1), after=(own4,))
    across2 = middle(far2)
    back1 = outer_out(home1)
    far3, home2 = relay((rest3, 1, got3, 1, 2), (rest2, 0, across2, 1, 1), after=(far2,))
    across3 = middle(far3)
    back2 = outer_out(home2)
    (home3,) = relay((rest3, 0, across3, 1, 1), after=(far3,))
    back3 = outer_out(home3)

    def total(own, got, across, back):
        return own.astype(F32) + got[0].astype(F32) + across[0].astype(F32) + back[0].astype(F32)

    weight_grad = jnp.concatenate(
        [
            total(own0, got0, across0, back0),
            total(own1, got1, across1, back1),
            total(own2, got2, across2, back2),
            total(own3, got3, across3, back3),
            own4.astype(F32) + sum(x.astype(F32) for x in arrived),
        ],
        axis=0,
    )
    input_grad = (
        near[0].astype(F32) + sib0[0].astype(F32) + xback[0].astype(F32)
    ).astype(BF16)
    return act, input_grad, weight_grad


def local_any(features, weight, rows_index, cotangent):
    tokens = features.shape[0]
    columns, depth, side = weight.shape
    per_column = depth // side
    scale = 1.0 / math.sqrt(tokens * lax.axis_size("replica"))
    whole = lax.all_gather(features, "shard", axis=1, tiled=True)
    block_rows = whole.shape[1] // side
    first = lax.axis_index("shard") * columns
    local_rows = lax.dynamic_slice_in_dim(rows_index, first, columns, 0)
    rows = rows_index.reshape(-1)
    step = math.gcd(columns, STEP)
    act, delta = forward(rows, [whole], weight, cotangent, 0, None, 0, (columns,), step)
    (part,) = dinput(rows, weight, [delta], 0, ((0,),), whole.shape[1], step)
    input_grad = lax.psum_scatter(part[0], "shard", scatter_dimension=1, tiled=True)
    blocks = whole.reshape(tokens, block_rows, side)[:, local_rows]
    grads = jnp.einsum(
        "qlpf,qlx->lpfx",
        blocks,
        delta.reshape(tokens, columns, side),
        preferred_element_type=F32,
    ).reshape(columns, per_column * side, side)
    weight_grad = lax.psum_scatter(grads, "replica", scatter_dimension=1, tiled=True) * scale
    return act, input_grad, weight_grad


def solution(mesh):
    placed = (P("replica", "shard"), P("shard", None, None), P(), P("replica", "shard"))
    fits = mesh.shape["replica"] == 8 and mesh.shape["shard"] == 4
    return jax.shard_map(
        local_line if fits else local_any,
        mesh=mesh,
        in_specs=placed,
        out_specs=(P("replica", "shard"), P("replica", "shard"), P("shard", "replica", None)),
        check_vma=False,
    )
```

```python
import functools
import math

import jax
import jax.numpy as jnp
from jax import lax
from jax.experimental import pallas as pl
from jax.experimental.pallas import tpu as pltpu
from jax.sharding import PartitionSpec as P

F32 = jnp.float32
BF16 = jnp.bfloat16
ANY = pl.BlockSpec(memory_space=pl.ANY)
PARAMS = pltpu.CompilerParams(
    dimension_semantics=("arbitrary",), vmem_limit_bytes=48 * 1024 * 1024
)
ALL = pltpu.CompilerParams(
    dimension_semantics=("arbitrary",), vmem_limit_bytes=60 * 1024 * 1024
)
FEW = pltpu.CompilerParams(vmem_limit_bytes=1024 * 1024)
STEP = 4


def copy_in(groups, buf, rows, tab, sems):
    copies = [pltpu.make_async_copy(rows, tab, sems.at[0])]
    top = 0
    for group in groups:
        at = 0
        for ref in group:
            height, width = ref.shape
            copies.append(
                pltpu.make_async_copy(
                    ref,
                    buf.at[pl.ds(top, height), pl.ds(at, width)],
                    sems.at[len(copies)],
                )
            )
            at += width
        top += height
    for copy in copies:
        copy.start()
    for copy in copies:
        copy.wait()


class Index:
    def __init__(self, tab, columns, per_column, fold, side):
        shard = lax.axis_index("shard")
        self.base = shard * columns
        self.flip = shard * fold
        self.tab, self.per_column, self.side = tab, per_column, side

    def block(self, col, k):
        return self.tab[(self.base + col) * self.per_column + k] ^ self.flip

    def lanes(self, col, k):
        return pl.ds(pl.multiple_of(self.block(col, k) * self.side, self.side), self.side)

    def gather(self, buf, col, ks):
        return jnp.concatenate([buf[:, self.lanes(col, k)] for k in ks], axis=1)


def staged_blocks(line):
    r = lax.axis_index("replica")
    z, y = r // 2, r % 2
    inner = (z == 1) | (z == 2)
    one, zero = jnp.int32(1), jnp.int32(0)
    order = [
        jnp.where(inner, one, zero),
        jnp.where(inner, zero, one),
        jnp.int32(2),
        jnp.int32(3),
    ]
    return [jnp.where(z >= line // 2, line - 1 - d, d) * 2 + y for d in order]


def forward_column(x, w, cot):
    pre = jnp.dot(x, w, preferred_element_type=F32)
    sig = 1.0 / (1.0 + jnp.exp(-pre))
    delta = (cot.astype(F32) * sig * (1.0 + pre * (1.0 - sig))).astype(BF16)
    return pre, sig, delta


def ranges(splits, step):
    out, start = [], 0
    for n in splits:
        out.append((start // step, (start + n) // step - 1))
        start += n
    return out


def held_at(lo, hi):
    return lambda i: jnp.clip(i, lo, hi) - lo


def forward_kernel(nf, columns, fold, copies, *refs):
    rows, feats = refs[0], refs[1 : 1 + nf]
    w_ref, cot_ref = refs[1 + nf : 3 + nf]
    buf, tab, sems = refs[-3:]
    act_ref, delta_ref, *cot_copies = refs[-5 - len(copies) : -3]
    step, depth, side = w_ref.shape
    per_column = depth // side
    here = pl.program_id(0)

    @pl.when(here == 0)
    def _():
        copy_in([feats], buf, rows, tab, sems)

    index = Index(tab, columns, per_column, fold, side)
    for i in range(step):
        x = index.gather(buf, here * step + i, range(per_column))
        lanes = slice(i * side, (i + 1) * side)
        pre, sig, delta = forward_column(x, w_ref[i], cot_ref[:, lanes])
        act_ref[:, lanes] = (pre * sig).astype(BF16)
        delta_ref[:, lanes] = delta
    for ref, (lo, hi) in zip(cot_copies, copies):

        @pl.when((here >= lo) & (here <= hi))
        def _(ref=ref):
            ref[...] = cot_ref[...]


def forward(rows, feats, weight, cotangent, fold, step, parts=(), after=()):
    tokens, hidden = cotangent.shape
    columns, depth, side = weight.shape
    width = sum(f.shape[1] for f in feats)
    args = [rows, *feats, weight, cotangent, *after]
    ins = [ANY] * (1 + len(feats)) + [
        pl.BlockSpec((step, depth, side), lambda i: (i, 0, 0)),
        pl.BlockSpec((tokens, step * side), lambda i: (0, i)),
    ]
    ins += [ANY] * (len(args) - len(ins))
    outs = [pl.BlockSpec((tokens, step * side), lambda i: (0, i))] * 2
    copies = ranges(parts, step)[1:]
    for lo, hi in copies:
        at = held_at(lo, hi)
        outs.append(pl.BlockSpec((tokens, step * side), lambda i, at=at: (0, at(i))))
    return pl.pallas_call(
        functools.partial(forward_kernel, len(feats), columns, fold, copies),
        grid=(columns // step,),
        in_specs=ins,
        out_specs=outs,
        scratch_shapes=[
            pltpu.VMEM((tokens, width), BF16),
            pltpu.SMEM(rows.shape, jnp.int32),
            pltpu.SemaphoreType.DMA((1 + len(feats),)),
        ],
        out_shape=[jax.ShapeDtypeStruct((tokens, hidden), BF16)] * 2
        + [jax.ShapeDtypeStruct((tokens, n * side), BF16) for n in parts[1:]],
        compiler_params=PARAMS,
        name="forward",
    )(*args)


def block_grads(index, buf, ks, col, delta, scale):
    side = index.side
    x = index.gather(buf, col, ks)
    grad = lax.dot_general(
        x, delta, (((0,), (0,)), ((), ())), preferred_element_type=F32
    )
    return [
        (grad[p * side : (p + 1) * side] * scale).astype(BF16) for p in range(len(ks))
    ]


def grads_kernel(nf, first, columns, fold, scale, last, *refs):
    rows, mine, other = refs[0], refs[1 : 1 + nf], refs[1 + nf : 1 + 2 * nf]
    w_ref, delta_ref, cot_ref = refs[1 + 2 * nf : 4 + 2 * nf]
    buf, tab, sems = refs[-3:]
    own_ref, rest_ref, *home = refs[-6 if last else -5 : -3]
    step, depth, side = w_ref.shape
    per_column = depth // side
    tokens = cot_ref.shape[0]
    here = pl.program_id(0)

    @pl.when(here == 0)
    def _():
        copy_in([mine, other], buf, rows, tab, sems)

    index = Index(tab, columns, per_column, fold, side)
    ks = staged_blocks(1 + rest_ref.shape[0])
    pair = buf.at[pl.ds(tokens, tokens), :]
    done = []
    for i in range(step):
        x = index.gather(pair, first + here * step + i, range(per_column))
        lanes = slice(i * side, (i + 1) * side)
        _, _, delta = forward_column(x, w_ref[i], cot_ref[:, lanes])
        done.append(jnp.concatenate([delta_ref[:, lanes], delta], axis=0))
    for i in range(step):
        blocks = block_grads(index, buf, ks, first + here * step + i, done[i], scale)
        own_ref[i] = blocks[0]
        for p, block in enumerate(blocks[1:]):
            rest_ref[p, i] = block
        if last:
            home[0][0, i] = blocks[1]


def grads(
    rows, mine, other, weight, delta, cot_other, skip, count, fold, first, line, scale, after=()
):
    tokens = delta.shape[0]
    columns, depth, side = weight.shape
    width = sum(f.shape[1] for f in mine)
    step = math.gcd(first, skip, count, STEP)
    base, skip = first // step, skip // step
    args = [rows, *mine, *other, weight, delta, cot_other, *after]
    ins = [ANY] * (1 + 2 * len(mine)) + [
        pl.BlockSpec((step, depth, side), lambda i: (base + i, 0, 0)),
        pl.BlockSpec((tokens, step * side), lambda i: (0, base + i)),
        pl.BlockSpec((tokens, step * side), lambda i: (0, skip + i)),
    ]
    ins += [ANY] * (len(args) - len(ins))
    one = jax.ShapeDtypeStruct((count, side, side), BF16)
    one_spec = pl.BlockSpec((step, side, side), lambda i: (i, 0, 0))
    last = first + count == columns
    piece = lambda n: jax.ShapeDtypeStruct((n, count, side, side), BF16)
    piece_spec = lambda n: pl.BlockSpec((n, step, side, side), lambda i: (0, i, 0, 0))
    sends, send_specs = [piece(line - 1)], [piece_spec(line - 1)]
    if last:
        sends.append(piece(1))
        send_specs.append(piece_spec(1))
    return pl.pallas_call(
        functools.partial(grads_kernel, len(mine), first, columns, fold, scale, last),
        grid=(count // step,),
        in_specs=ins,
        out_specs=[one_spec, *send_specs],
        scratch_shapes=[
            pltpu.VMEM((2 * tokens, width), BF16),
            pltpu.SMEM(rows.shape, jnp.int32),
            pltpu.SemaphoreType.DMA((1 + 2 * len(mine),)),
        ],
        out_shape=[one, *sends],
        compiler_params=PARAMS,
        name="grads",
    )(*args)


def dinput_kernel(nd, fold, groups, *refs):
    rows, deltas, w_ref = refs[0], refs[1 : 1 + nd], refs[1 + nd]
    buf, acc, tab, sems = refs[-4:]
    outs = refs[-4 - len(groups) : -4]
    step, depth, side = w_ref.shape
    per_column = depth // side
    here = pl.program_id(0)

    @pl.when(here == 0)
    def _():
        copy_in([deltas], buf, rows, tab, sems)
        acc[...] = jnp.zeros_like(acc)

    index = Index(tab, buf.shape[1] // side, per_column, fold, side)
    for i in range(step):
        col = here * step + i
        d = buf[:, pl.ds(pl.multiple_of(col * side, side), side)]
        g = lax.dot_general(
            d, w_ref[i], (((1,), (1,)), ((), ())), preferred_element_type=F32
        )
        for k in range(per_column):
            acc[index.block(col, k)] += g[:, k * side : (k + 1) * side]

    @pl.when(here == pl.num_programs(0) - 1)
    def _():
        for out, group in zip(outs, groups):
            blocks = out.shape[2] // side
            for n, piece in enumerate(group):
                for b in range(blocks):
                    out[n, :, b * side : (b + 1) * side] = acc[piece * blocks + b].astype(BF16)


def dinput(rows, weight, deltas, fold, groups, width, step, after=()):
    tokens = deltas[0].shape[0]
    columns, depth, side = weight.shape
    pieces = sum(len(g) for g in groups)
    shapes = [(len(g), tokens, width) for g in groups]
    return pl.pallas_call(
        functools.partial(dinput_kernel, len(deltas), fold, groups),
        grid=(columns // step,),
        in_specs=[ANY] * (1 + len(deltas))
        + [pl.BlockSpec((step, depth, side), lambda i: (i, 0, 0))]
        + [ANY] * len(after),
        out_specs=[pl.BlockSpec(s, lambda i: (0, 0, 0)) for s in shapes],
        scratch_shapes=[
            pltpu.VMEM((tokens, columns * side), BF16),
            pltpu.VMEM((pieces * width // side, tokens, side), F32),
            pltpu.SMEM(rows.shape, jnp.int32),
            pltpu.SemaphoreType.DMA((1 + len(deltas),)),
        ],
        out_shape=[jax.ShapeDtypeStruct(s, BF16) for s in shapes],
        compiler_params=PARAMS,
        name="dinput",
    )(rows, *deltas, weight, *after)


def relay_kernel(jobs, *refs):
    outs = refs[-len(jobs) :]
    for n, (a_at, b_at, count) in enumerate(jobs):
        a, b = refs[2 * n], refs[2 * n + 1]
        for i in range(count):
            outs[n][i] = (a[a_at + i].astype(F32) + b[b_at + i].astype(F32)).astype(BF16)


def relay(*jobs, after=()):
    args, ins, outs, shapes, cuts = [], [], [], [], []
    steps = 2
    for a, a_at, b, b_at, count in jobs:
        part = (a.shape[1] // steps,) + a.shape[2:]
        zeros = (0,) * (a.ndim - 2)
        for x in (a, b):
            args.append(x)
            ins.append(pl.BlockSpec(x.shape[:1] + part, lambda i, z=zeros: (0, i) + z))
        outs.append(pl.BlockSpec((count,) + part, lambda i, z=zeros: (0, i) + z))
        shapes.append(jax.ShapeDtypeStruct((count,) + a.shape[1:], BF16))
        cuts.append((a_at, b_at, count))

    def kernel(*refs):
        relay_kernel(cuts, *refs[: len(args)], *refs[len(args) + len(after) :])

    return pl.pallas_call(
        kernel,
        grid=(steps,),
        in_specs=ins + [ANY] * len(after),
        out_specs=outs,
        out_shape=shapes,
        compiler_params=PARAMS,
        name="relay",
    )(*args, *after)


def cut_kernel(x_ref, whole_ref, rows_ref, out_ref, copy_ref):
    del rows_ref
    out_ref[...] = x_ref[...]
    copy_ref[...] = whole_ref[...]


def cut(x, width, whole, rows):
    return pl.pallas_call(
        cut_kernel,
        grid=(1,),
        in_specs=[
            pl.BlockSpec((x.shape[0], width), lambda i: (0, 0)),
            pl.BlockSpec(whole.shape, lambda i: (0, 0)),
            ANY,
        ],
        out_specs=[
            pl.BlockSpec((x.shape[0], width), lambda i: (0, 0)),
            pl.BlockSpec(whole.shape, lambda i: (0, 0)),
        ],
        out_shape=[
            jax.ShapeDtypeStruct((x.shape[0], width), x.dtype),
            jax.ShapeDtypeStruct(whole.shape, whole.dtype),
        ],
        compiler_params=ALL,
        name="cut",
    )(x, whole, rows)


def gate_kernel(*refs):
    del refs


def gate(x, *after):
    return pl.pallas_call(
        gate_kernel,
        in_specs=[ANY] * (1 + len(after)),
        out_specs=ANY,
        out_shape=jax.ShapeDtypeStruct(x.shape, x.dtype),
        input_output_aliases={0: 0},
        compiler_params=FEW,
        name="gate",
    )(x, *after)


def local_line(features, weight, rows_index, cotangent):
    tokens, held = features.shape
    columns, depth, side = weight.shape
    per_column = depth // side
    replicas, shards = lax.axis_size("replica"), lax.axis_size("shard")
    scale = 1.0 / math.sqrt(tokens * replicas)
    rows = rows_index.reshape(-1)
    fold = held // side
    line = replicas // 2

    def permute(axis, links):
        return lambda x: lax.ppermute(x, axis, links)

    def along(steps):
        return permute("replica", [(a * 2 + p, b * 2 + p) for a, b in steps for p in range(2)])

    cores = permute("shard", [(i, i ^ 1) for i in range(shards)])
    chips = permute("shard", [(i, i ^ 2) for i in range(shards)])
    pairs = permute("replica", [(i, i ^ 1) for i in range(replicas)])
    outer_in = along([(0, 1), (3, 2)])
    middle = along([(1, 2), (2, 1)])
    outer_out = along([(1, 0), (2, 3)])
    beyond = along([(1, 3), (2, 0)])

    sizes = [c * columns // 32 for c in (8, 8, 6, 6, 4)]
    firsts = [sum(sizes[:n]) for n in range(len(sizes))]
    parts = [sizes[0], sizes[1], sizes[2] + sizes[3] + sizes[4]]
    places = [(0, 0), (1, 0), (2, 0), (2, sizes[2]), (2, sizes[2] + sizes[3])]

    f0 = features
    f2 = chips(f0)
    cot0, sent = cut(cotangent, parts[0] * side, f0, rows)
    u0 = pairs(sent)
    c0 = pairs(cot0)
    f1 = cores(f0)
    f3 = cores(f2)
    u1 = cores(u0)
    u2 = chips(u0)
    mine = [f0, f1, f2, f3]
    act, delta, cot1, cot2 = forward(rows, mine, weight, cotangent, fold, STEP, parts)
    c1, c2 = pairs(cot1), pairs(cot2)
    cs = [c0, c1, c2]
    u2 = gate(u2, delta, c0)
    u3 = cores(u2)
    other = [u0, u1, u2, u3]

    def chunk(n, *after):
        part, skip = places[n]
        return grads(
            rows, mine, other, weight, delta, cs[part], skip, sizes[n], fold, firsts[n],
            line, scale, after,
        )

    own0, rest0 = chunk(0)
    got0 = outer_in(rest0)
    own1, rest1 = chunk(1, own0)
    got1 = outer_in(rest1)
    near, away0, away1 = dinput(
        rows, weight, [delta], fold, ((0, 2), (1,), (3,)), held, STEP, (own1,)
    )
    sib0, sib1 = cores(away0), cores(away1)
    (far0,) = relay((rest0, 1, got0, 1, 2), after=(near,))
    across0 = middle(far0)
    own2, rest2 = chunk(2, far0)
    got2 = outer_in(rest2)
    (xsum,) = relay((near, 1, sib1, 0, 1), after=(own2,))
    xback = chips(xsum)
    far1, home0 = relay((rest1, 1, got1, 1, 2), (rest0, 0, across0, 1, 1), after=(xsum,))
    across1 = middle(far1)
    back0 = outer_out(home0)
    own3, rest3 = chunk(3, far1)
    got3 = outer_in(rest3)
    far2, home1 = relay((rest2, 1, got2, 1, 2), (rest1, 0, across1, 1, 1), after=(own3,))
    across2 = middle(far2)
    back1 = outer_out(home1)
    own4, rest4, home4 = chunk(4, far2)
    got4 = outer_in(rest4)
    back4 = outer_out(home4)
    far3, home2 = relay((rest3, 1, got3, 1, 2), (rest2, 0, across2, 1, 1), after=(own4,))
    across3 = middle(far3)
    back2 = outer_out(home2)
    last0, last1 = relay((rest4, 1, got4, 1, 1), (rest4, 2, got4, 2, 1), after=(far3,))
    near4, far4 = middle(last0), beyond(last1)
    (home3,) = relay((rest3, 0, across3, 1, 1), after=(last0,))
    back3 = outer_out(home3)

    def total(own, got, *more):
        return own.astype(F32) + got[0].astype(F32) + sum(x[0].astype(F32) for x in more)

    weight_grad = jnp.concatenate(
        [
            total(own0, got0, across0, back0),
            total(own1, got1, across1, back1),
            total(own2, got2, across2, back2),
            total(own3, got3, across3, back3),
            total(own4, got4, near4, far4, back4),
        ],
        axis=0,
    )
    input_grad = (
        near[0].astype(F32) + sib0[0].astype(F32) + xback[0].astype(F32)
    ).astype(BF16)
    return act, input_grad, weight_grad


def local_any(features, weight, rows_index, cotangent):
    tokens = features.shape[0]
    columns, depth, side = weight.shape
    per_column = depth // side
    scale = 1.0 / math.sqrt(tokens * lax.axis_size("replica"))
    whole = lax.all_gather(features, "shard", axis=1, tiled=True)
    block_rows = whole.shape[1] // side
    first = lax.axis_index("shard") * columns
    local_rows = lax.dynamic_slice_in_dim(rows_index, first, columns, 0)
    rows = rows_index.reshape(-1)
    step = math.gcd(columns, STEP)
    act, delta = forward(rows, [whole], weight, cotangent, 0, step)
    (part,) = dinput(rows, weight, [delta], 0, ((0,),), whole.shape[1], step)
    input_grad = lax.psum_scatter(part[0], "shard", scatter_dimension=1, tiled=True)
    blocks = whole.reshape(tokens, block_rows, side)[:, local_rows]
    grads = jnp.einsum(
        "qlpf,qlx->lpfx",
        blocks,
        delta.reshape(tokens, columns, side),
        preferred_element_type=F32,
    ).reshape(columns, per_column * side, side)
    weight_grad = lax.psum_scatter(grads, "replica", scatter_dimension=1, tiled=True) * scale
    return act, input_grad, weight_grad


def solution(mesh):
    placed = (P("replica", "shard"), P("shard", None, None), P(), P("replica", "shard"))
    fits = mesh.shape["replica"] == 8 and mesh.shape["shard"] == 4
    return jax.shard_map(
        local_line if fits else local_any,
        mesh=mesh,
        in_specs=placed,
        out_specs=(P("replica", "shard"), P("replica", "shard"), P("shard", "replica", None)),
        check_vma=False,
    )
```

```python
import functools
import math

import jax
import jax.numpy as jnp
from jax import lax
from jax.experimental import pallas as pl
from jax.experimental.pallas import tpu as pltpu
from jax.sharding import PartitionSpec as P

F32 = jnp.float32
BF16 = jnp.bfloat16
ANY = pl.BlockSpec(memory_space=pl.ANY)
PARAMS = pltpu.CompilerParams(
    dimension_semantics=("arbitrary",), vmem_limit_bytes=36 * 1024 * 1024
)
ALL = pltpu.CompilerParams(
    dimension_semantics=("arbitrary",), vmem_limit_bytes=60 * 1024 * 1024
)
FEW = pltpu.CompilerParams(vmem_limit_bytes=1024 * 1024)
STEP = 4


def copy_in(groups, buf, rows, tab, sems):
    copies = [pltpu.make_async_copy(rows, tab, sems.at[0])]
    top = 0
    for group in groups:
        at = 0
        for ref in group:
            height, width = ref.shape
            copies.append(
                pltpu.make_async_copy(
                    ref,
                    buf.at[pl.ds(top, height), pl.ds(at, width)],
                    sems.at[len(copies)],
                )
            )
            at += width
        top += height
    for copy in copies:
        copy.start()
    for copy in copies:
        copy.wait()


class Index:
    def __init__(self, tab, columns, per_column, fold, side):
        shard = lax.axis_index("shard")
        self.base = shard * columns
        self.flip = shard * fold
        self.tab, self.per_column, self.side = tab, per_column, side

    def block(self, col, k):
        return self.tab[(self.base + col) * self.per_column + k] ^ self.flip

    def lanes(self, col, k):
        return pl.ds(pl.multiple_of(self.block(col, k) * self.side, self.side), self.side)

    def gather(self, buf, col, ks):
        return jnp.concatenate([buf[:, self.lanes(col, k)] for k in ks], axis=1)


def staged_blocks(line):
    r = lax.axis_index("replica")
    z, y = r // 2, r % 2
    inner = (z == 1) | (z == 2)
    one, zero = jnp.int32(1), jnp.int32(0)
    order = [
        jnp.where(inner, one, zero),
        jnp.where(inner, zero, one),
        jnp.int32(2),
        jnp.int32(3),
    ]
    return [jnp.where(z >= line // 2, line - 1 - d, d) * 2 + y for d in order]


def forward_column(x, w, cot):
    pre = jnp.dot(x, w, preferred_element_type=F32)
    sig = 1.0 / (1.0 + jnp.exp(-pre))
    delta = (cot.astype(F32) * sig * (1.0 + pre * (1.0 - sig))).astype(BF16)
    return pre, sig, delta


def ranges(splits, step):
    out, start = [], 0
    for n in splits:
        out.append((start // step, (start + n) // step - 1))
        start += n
    return out


def held_at(lo, hi):
    return lambda i: jnp.clip(i, lo, hi) - lo


def forward_kernel(nf, first, columns, fold, copies, ahead, *refs):
    rows, feats = refs[0], refs[1 : 1 + nf]
    w_ref, cot_ref, cot_ahead_ref = refs[1 + nf : 4 + nf]
    buf, tab, sems = refs[-3:]
    act_ref, delta_ref, *cot_copies = refs[-5 - len(copies) - ahead : -3]
    step, depth, side = w_ref.shape
    per_column = depth // side
    here = pl.program_id(0)

    @pl.when(here == 0)
    def _():
        copy_in([feats], buf, rows, tab, sems)

    index = Index(tab, columns, per_column, fold, side)
    for i in range(step):
        x = index.gather(buf, first + here * step + i, range(per_column))
        lanes = slice(i * side, (i + 1) * side)
        pre, sig, delta = forward_column(x, w_ref[i], cot_ref[:, lanes])
        act_ref[:, lanes] = (pre * sig).astype(BF16)
        delta_ref[:, lanes] = delta
    for ref, (lo, hi) in zip(cot_copies, copies):

        @pl.when((here >= lo) & (here <= hi))
        def _(ref=ref):
            ref[...] = cot_ref[...]

    if ahead:
        cot_copies[-1][...] = cot_ahead_ref[...]


def forward(rows, feats, weight, cotangent, fold, act, first, parts, copied, ahead, step, after=()):
    tokens, hidden = cotangent.shape
    columns, depth, side = weight.shape
    width = sum(f.shape[1] for f in feats)
    count = sum(parts)
    base = first // step
    jump = base + count // step if ahead else base
    args = [rows, *feats, weight, cotangent, cotangent]
    wide = lambda at: pl.BlockSpec((tokens, step * side), lambda i: (0, at + i))
    ins = [ANY] * (1 + len(feats)) + [
        pl.BlockSpec((step, depth, side), lambda i: (base + i, 0, 0)),
        wide(base),
        wide(jump),
    ]
    aliases = {}
    if act is not None:
        aliases = {len(args): 0}
        args.append(act)
    args += after
    ins += [ANY] * (len(args) - len(ins))
    outs = [wide(base), wide(0)]
    spans = ranges(parts, step)
    copies = [spans[n] for n in copied]
    for lo, hi in copies:
        at = held_at(lo, hi)
        outs.append(pl.BlockSpec((tokens, step * side), lambda i, at=at: (0, at(i))))
    sizes = [parts[n] for n in copied]
    if ahead:
        outs.append(wide(0))
        sizes.append(count)
    return pl.pallas_call(
        functools.partial(forward_kernel, len(feats), first, columns, fold, copies, ahead),
        grid=(count // step,),
        in_specs=ins,
        out_specs=outs,
        scratch_shapes=[
            pltpu.VMEM((tokens, width), BF16),
            pltpu.SMEM(rows.shape, jnp.int32),
            pltpu.SemaphoreType.DMA((1 + len(feats),)),
        ],
        out_shape=[
            jax.ShapeDtypeStruct((tokens, hidden), BF16),
            jax.ShapeDtypeStruct((tokens, count * side), BF16),
        ]
        + [jax.ShapeDtypeStruct((tokens, n * side), BF16) for n in sizes],
        input_output_aliases=aliases,
        compiler_params=PARAMS,
        name="forward",
    )(*args)


def block_grads(index, buf, ks, col, delta, scale):
    side = index.side
    x = index.gather(buf, col, ks)
    grad = lax.dot_general(
        x, delta, (((0,), (0,)), ((), ())), preferred_element_type=F32
    )
    return [
        (grad[p * side : (p + 1) * side] * scale).astype(BF16) for p in range(len(ks))
    ]


def grads_kernel(nf, first, columns, fold, scale, *refs):
    rows, mine, other = refs[0], refs[1 : 1 + nf], refs[1 + nf : 1 + 2 * nf]
    w_ref, delta_ref, cot_ref = refs[1 + 2 * nf : 4 + 2 * nf]
    buf, tab, sems = refs[-3:]
    own_ref, rest_ref = refs[-5:-3]
    step, depth, side = w_ref.shape
    per_column = depth // side
    tokens = cot_ref.shape[0]
    here = pl.program_id(0)

    @pl.when(here == 0)
    def _():
        copy_in([mine, other], buf, rows, tab, sems)

    index = Index(tab, columns, per_column, fold, side)
    ks = staged_blocks(1 + rest_ref.shape[0])
    pair = buf.at[pl.ds(tokens, tokens), :]
    done = []
    for i in range(step):
        x = index.gather(pair, first + here * step + i, range(per_column))
        lanes = slice(i * side, (i + 1) * side)
        _, _, delta = forward_column(x, w_ref[i], cot_ref[:, lanes])
        done.append(jnp.concatenate([delta_ref[:, lanes], delta], axis=0))
    for i in range(step):
        blocks = block_grads(index, buf, ks, first + here * step + i, done[i], scale)
        own_ref[i] = blocks[0]
        for p, block in enumerate(blocks[1:]):
            rest_ref[p, i] = block


def grads(
    rows, mine, other, weight, delta, at, cot_other, skip, count, fold, first, line, scale,
    after=(),
):
    tokens = delta.shape[0]
    columns, depth, side = weight.shape
    width = sum(f.shape[1] for f in mine)
    step = math.gcd(first, at, skip, count, STEP)
    base, at, skip = first // step, at // step, skip // step
    args = [rows, *mine, *other, weight, delta, cot_other, *after]
    ins = [ANY] * (1 + 2 * len(mine)) + [
        pl.BlockSpec((step, depth, side), lambda i: (base + i, 0, 0)),
        pl.BlockSpec((tokens, step * side), lambda i: (0, at + i)),
        pl.BlockSpec((tokens, step * side), lambda i: (0, skip + i)),
    ]
    ins += [ANY] * (len(args) - len(ins))
    return pl.pallas_call(
        functools.partial(grads_kernel, len(mine), first, columns, fold, scale),
        grid=(count // step,),
        in_specs=ins,
        out_specs=[
            pl.BlockSpec((step, side, side), lambda i: (i, 0, 0)),
            pl.BlockSpec((line - 1, step, side, side), lambda i: (0, i, 0, 0)),
        ],
        scratch_shapes=[
            pltpu.VMEM((2 * tokens, width), BF16),
            pltpu.SMEM(rows.shape, jnp.int32),
            pltpu.SemaphoreType.DMA((1 + 2 * len(mine),)),
        ],
        out_shape=[
            jax.ShapeDtypeStruct((count, side, side), BF16),
            jax.ShapeDtypeStruct((line - 1, count, side, side), BF16),
        ],
        compiler_params=PARAMS,
        name="grads",
    )(*args)


def dinput_kernel(nd, fold, groups, *refs):
    rows, deltas, w_ref = refs[0], refs[1 : 1 + nd], refs[1 + nd]
    buf, acc, tab, sems = refs[-4:]
    outs = refs[-4 - len(groups) : -4]
    step, depth, side = w_ref.shape
    per_column = depth // side
    here = pl.program_id(0)

    @pl.when(here == 0)
    def _():
        copy_in([deltas], buf, rows, tab, sems)
        acc[...] = jnp.zeros_like(acc)

    index = Index(tab, buf.shape[1] // side, per_column, fold, side)
    for i in range(step):
        col = here * step + i
        d = buf[:, pl.ds(pl.multiple_of(col * side, side), side)]
        g = lax.dot_general(
            d, w_ref[i], (((1,), (1,)), ((), ())), preferred_element_type=F32
        )
        for k in range(per_column):
            acc[index.block(col, k)] += g[:, k * side : (k + 1) * side]

    @pl.when(here == pl.num_programs(0) - 1)
    def _():
        for out, group in zip(outs, groups):
            blocks = out.shape[2] // side
            for n, piece in enumerate(group):
                for b in range(blocks):
                    out[n, :, b * side : (b + 1) * side] = acc[piece * blocks + b].astype(BF16)


def dinput(rows, weight, deltas, fold, groups, width, step, after=()):
    tokens = deltas[0].shape[0]
    columns, depth, side = weight.shape
    pieces = sum(len(g) for g in groups)
    shapes = [(len(g), tokens, width) for g in groups]
    return pl.pallas_call(
        functools.partial(dinput_kernel, len(deltas), fold, groups),
        grid=(columns // step,),
        in_specs=[ANY] * (1 + len(deltas))
        + [pl.BlockSpec((step, depth, side), lambda i: (i, 0, 0))]
        + [ANY] * len(after),
        out_specs=[pl.BlockSpec(s, lambda i: (0, 0, 0)) for s in shapes],
        scratch_shapes=[
            pltpu.VMEM((tokens, columns * side), BF16),
            pltpu.VMEM((pieces * width // side, tokens, side), F32),
            pltpu.SMEM(rows.shape, jnp.int32),
            pltpu.SemaphoreType.DMA((1 + len(deltas),)),
        ],
        out_shape=[jax.ShapeDtypeStruct(s, BF16) for s in shapes],
        compiler_params=PARAMS,
        name="dinput",
    )(rows, *deltas, weight, *after)


def relay_kernel(jobs, *refs):
    outs = refs[-len(jobs) :]
    refs = list(refs)
    for out, parts in zip(outs, jobs):
        at = 0
        for a_at, b_at, count in parts:
            a = refs.pop(0)
            b = None if b_at is None else refs.pop(0)
            wide = a.shape[1]
            for i in range(count):
                value = a[a_at + i]
                if b is not None:
                    value = (value.astype(F32) + b[b_at + i].astype(F32)).astype(BF16)
                out[i, at : at + wide] = value
            at += wide


def relay(*jobs, after=()):
    args, shapes, cuts = [], [], []
    for parts in jobs:
        cuts.append([])
        wide = 0
        for a, a_at, b, b_at, count in parts:
            args += [a] if b is None else [a, b]
            cuts[-1].append((a_at, None if b is None else b_at, count))
            wide += a.shape[1]
        shapes.append((count, wide) + a.shape[2:])
    used = len(args)

    def kernel(*refs):
        relay_kernel(cuts, *refs[:used], *refs[used + len(after) :])

    whole = lambda shape: pl.BlockSpec(shape, lambda i: (0,) * len(shape))
    return pl.pallas_call(
        kernel,
        grid=(1,),
        in_specs=[whole(x.shape) for x in args] + [ANY] * len(after),
        out_specs=[whole(x) for x in shapes],
        out_shape=[jax.ShapeDtypeStruct(x, BF16) for x in shapes],
        compiler_params=PARAMS,
        name="relay",
    )(*args, *after)


def cut_kernel(x_ref, out_ref):
    out_ref[...] = x_ref[...]


def cut(x, width):
    spec = pl.BlockSpec((x.shape[0], width), lambda i: (0, 0))
    return pl.pallas_call(
        cut_kernel,
        grid=(1,),
        in_specs=[spec],
        out_specs=spec,
        out_shape=jax.ShapeDtypeStruct((x.shape[0], width), x.dtype),
        compiler_params=ALL,
        name="cut",
    )(x)


def total_kernel(chunks, *refs):
    out_ref = refs[-1]
    refs = list(refs)
    at = 0
    for count, starts in chunks:
        value = 0.0
        for start in starts:
            ref = refs.pop(0)
            part = ref[0, start : start + count] if len(ref.shape) == 4 else ref[...]
            value = value + part.astype(F32)
        out_ref[at : at + count] = value
        at += count


def total(whole, first, columns, chunks, after=()):
    chunks = [[t if isinstance(t, tuple) else (t, 0) for t in terms] for terms in chunks]
    sizes = [(terms[0][0].shape[0], [start for _, start in terms]) for terms in chunks]
    count = sum(n for n, _ in sizes)
    side = chunks[0][0][0].shape[1]
    base = first // count
    args = [t for terms in chunks for t, _ in terms]
    ins = [
        pl.BlockSpec((1,) + t.shape[1:], lambda i: (0, 0, 0, 0))
        if t.ndim == 4
        else pl.BlockSpec(t.shape, lambda i: (0, 0, 0))
        for t in args
    ]
    used = len(args)
    aliases = {}
    if whole is not None:
        aliases = {len(args): 0}
        args.append(whole)
    args += after

    def kernel(*refs):
        total_kernel(sizes, *refs[:used], refs[-1])

    return pl.pallas_call(
        kernel,
        grid=(1,),
        in_specs=ins + [ANY] * (len(args) - len(ins)),
        out_specs=pl.BlockSpec((count, side, side), lambda i: (base, 0, 0)),
        out_shape=jax.ShapeDtypeStruct((columns, side, side), F32),
        input_output_aliases=aliases,
        compiler_params=PARAMS,
        name="total",
    )(*args)


def gate_kernel(*refs):
    del refs


def gate(x, *after):
    return pl.pallas_call(
        gate_kernel,
        in_specs=[ANY] * (1 + len(after)),
        out_specs=ANY,
        out_shape=jax.ShapeDtypeStruct(x.shape, x.dtype),
        input_output_aliases={0: 0},
        compiler_params=FEW,
        name="gate",
    )(x, *after)


def local_line(features, weight, rows_index, cotangent):
    tokens, held = features.shape
    columns, depth, side = weight.shape
    per_column = depth // side
    replicas, shards = lax.axis_size("replica"), lax.axis_size("shard")
    scale = 1.0 / math.sqrt(tokens * replicas)
    rows = rows_index.reshape(-1)
    fold = held // side
    line = replicas // 2

    def permute(axis, links):
        return lambda x: lax.ppermute(x, axis, links)

    def along(steps):
        return permute("replica", [(a * 2 + p, b * 2 + p) for a, b in steps for p in range(2)])

    cores = permute("shard", [(i, i ^ 1) for i in range(shards)])
    chips = permute("shard", [(i, i ^ 2) for i in range(shards)])
    pairs = permute("replica", [(i, i ^ 1) for i in range(replicas)])
    outer_in = along([(0, 1), (3, 2)])
    middle = along([(1, 2), (2, 1)])
    outer_out = along([(1, 0), (2, 3)])
    beyond = along([(1, 3), (2, 0)])

    sizes = [c * columns // 32 for c in (8, 8, 6, 6, 4)]
    firsts = [sum(sizes[:n]) for n in range(len(sizes))]
    parts = [sizes[0], sizes[1], sizes[2] + sizes[3] + sizes[4]]

    f0 = features
    f2 = chips(f0)
    u0 = pairs(f0)
    cot0 = cut(cotangent, parts[0] * side)
    f2 = gate(f2, cot0, rows)
    c0 = pairs(cot0)
    f1 = cores(f0)
    f3 = cores(f2)
    u1 = cores(u0)
    u2 = chips(u0)
    mine = [f0, f1, f2, f3]
    act, delta0, cot1, cot2 = forward(
        rows, mine, weight, cotangent, fold, None, 0, parts[:2], (1,), True, STEP
    )
    c1, c2 = pairs(cot1), pairs(cot2)
    u2 = gate(u2, delta0, c0)
    u3 = cores(u2)
    other = [u0, u1, u2, u3]

    def chunk(n, delta, cot, *after):
        half = firsts[n] - firsts[2] if n >= 2 else firsts[n]
        return grads(
            rows, mine, other, weight, delta, half, cot, half if n >= 2 else 0, sizes[n], fold,
            firsts[n], line, scale, after,
        )

    own0, rest0 = chunk(0, delta0, c0)
    got0 = outer_in(rest0)
    act, delta1 = forward(
        rows, mine, weight, cotangent, fold, act, firsts[2], parts[2:], (), False, STEP, (own0,)
    )
    own1, rest1 = chunk(1, delta0, c1, delta1)
    got1 = outer_in(rest1)
    near, away0, away1 = dinput(
        rows, weight, [delta0, delta1], fold, ((0, 2), (1,), (3,)), held, STEP, (own1,)
    )
    sib0, sib1 = cores(away0), cores(away1)
    (far0,) = relay([(rest0, 1, got0, 1, 2)], after=(near,))
    across0 = middle(far0)
    own2, rest2 = chunk(2, delta1, c2, far0)
    got2 = outer_in(rest2)
    (far1,) = relay([(rest1, 1, got1, 1, 2)], after=(own2,))
    across1 = middle(far1)
    own3, rest3 = chunk(3, delta1, c2, far1, across0)
    got3 = outer_in(rest3)
    (xsum,) = relay([(near, 1, sib1, 0, 1)], after=(own3, sib0))
    xback = chips(xsum)
    far2, home0 = relay(
        [(rest2, 1, got2, 1, 2)],
        [(rest0, 0, across0, 1, 1), (rest1, 0, across1, 1, 1)],
        after=(xsum,),
    )
    across2 = middle(far2)
    back0 = outer_out(home0)
    own4, rest4 = chunk(4, delta1, c2, far2)
    got4 = outer_in(rest4)
    third0, third1, home1 = relay(
        [(rest3, 1, got3, 1, 1)],
        [(rest3, 2, got3, 2, 1)],
        [(rest2, 0, across2, 1, 1), (rest3, 0, None, 0, 1), (rest4, 0, None, 0, 1)],
        after=(own4, xback),
    )
    near3, far3 = middle(third0), beyond(third1)
    back1 = outer_out(home1)
    last0, last1 = relay(
        [(rest4, 1, got4, 1, 1)], [(rest4, 2, got4, 2, 1)], after=(third0, back0)
    )
    near4, far4 = middle(last0), beyond(last1)
    grad = total(
        None,
        firsts[0],
        columns,
        [[own0, got0, across0, back0], [own1, got1, across1, (back0, sizes[0])]],
        (last0,),
    )
    weight_grad = total(
        grad,
        firsts[2],
        columns,
        [
            [own2, got2, across2, back1],
            [own3, got3, near3, far3, (back1, sizes[2])],
            [own4, got4, near4, far4, (back1, sizes[2] + sizes[3])],
        ],
    )
    input_grad = (
        near[0].astype(F32) + sib0[0].astype(F32) + xback[0].astype(F32)
    ).astype(BF16)
    return act, input_grad, weight_grad


def local_any(features, weight, rows_index, cotangent):
    tokens = features.shape[0]
    columns, depth, side = weight.shape
    per_column = depth // side
    scale = 1.0 / math.sqrt(tokens * lax.axis_size("replica"))
    whole = lax.all_gather(features, "shard", axis=1, tiled=True)
    block_rows = whole.shape[1] // side
    first = lax.axis_index("shard") * columns
    local_rows = lax.dynamic_slice_in_dim(rows_index, first, columns, 0)
    rows = rows_index.reshape(-1)
    step = math.gcd(columns, STEP)
    act, delta = forward(
        rows, [whole], weight, cotangent, 0, None, 0, (columns,), (), False, step
    )
    (part,) = dinput(rows, weight, [delta], 0, ((0,),), whole.shape[1], step)
    input_grad = lax.psum_scatter(part[0], "shard", scatter_dimension=1, tiled=True)
    blocks = whole.reshape(tokens, block_rows, side)[:, local_rows]
    grads = jnp.einsum(
        "qlpf,qlx->lpfx",
        blocks,
        delta.reshape(tokens, columns, side),
        preferred_element_type=F32,
    ).reshape(columns, per_column * side, side)
    weight_grad = lax.psum_scatter(grads, "replica", scatter_dimension=1, tiled=True) * scale
    return act, input_grad, weight_grad


def solution(mesh):
    placed = (P("replica", "shard"), P("shard", None, None), P(), P("replica", "shard"))
    fits = mesh.shape["replica"] == 8 and mesh.shape["shard"] == 4
    return jax.shard_map(
        local_line if fits else local_any,
        mesh=mesh,
        in_specs=placed,
        out_specs=(P("replica", "shard"), P("replica", "shard"), P("shard", "replica", None)),
        check_vma=False,
    )
```

```python
import functools
import math

import jax
import jax.numpy as jnp
from jax import lax
from jax.experimental import pallas as pl
from jax.experimental.pallas import tpu as pltpu
from jax.sharding import PartitionSpec as P

F32 = jnp.float32
BF16 = jnp.bfloat16
ANY = pl.BlockSpec(memory_space=pl.ANY)
PARAMS = pltpu.CompilerParams(
    dimension_semantics=("arbitrary",), vmem_limit_bytes=28 * 1024 * 1024
)
ALL = pltpu.CompilerParams(
    dimension_semantics=("arbitrary",), vmem_limit_bytes=60 * 1024 * 1024
)
FEW = pltpu.CompilerParams(vmem_limit_bytes=1024 * 1024)
STEP = 4


def copy_in(groups, buf, rows, tab, sems):
    copies = [pltpu.make_async_copy(rows, tab, sems.at[0])]
    top = 0
    for group in groups:
        at = 0
        for ref in group:
            height, width = ref.shape
            copies.append(
                pltpu.make_async_copy(
                    ref,
                    buf.at[pl.ds(top, height), pl.ds(at, width)],
                    sems.at[len(copies)],
                )
            )
            at += width
        top += height
    for copy in copies:
        copy.start()
    for copy in copies:
        copy.wait()


class Index:
    def __init__(self, tab, columns, per_column, fold, side):
        shard = lax.axis_index("shard")
        self.base = shard * columns
        self.flip = shard * fold
        self.tab, self.per_column, self.side = tab, per_column, side

    def block(self, col, k):
        return self.tab[(self.base + col) * self.per_column + k] ^ self.flip

    def lanes(self, col, k):
        return pl.ds(pl.multiple_of(self.block(col, k) * self.side, self.side), self.side)

    def gather(self, buf, col, ks):
        return jnp.concatenate([buf[:, self.lanes(col, k)] for k in ks], axis=1)


def staged_blocks(line):
    r = lax.axis_index("replica")
    z, y = r // 2, r % 2
    inner = (z == 1) | (z == 2)
    one, zero = jnp.int32(1), jnp.int32(0)
    order = [
        jnp.where(inner, one, zero),
        jnp.where(inner, zero, one),
        jnp.int32(2),
        jnp.int32(3),
    ]
    return [jnp.where(z >= line // 2, line - 1 - d, d) * 2 + y for d in order]


def forward_column(x, w, cot):
    pre = jnp.dot(x, w, preferred_element_type=F32)
    sig = 1.0 / (1.0 + jnp.exp(-pre))
    delta = (cot.astype(F32) * sig * (1.0 + pre * (1.0 - sig))).astype(BF16)
    return pre, sig, delta


def ranges(splits, step):
    out, start = [], 0
    for n in splits:
        out.append((start // step, (start + n) // step - 1))
        start += n
    return out


def held_at(lo, hi):
    return lambda i: jnp.clip(i, lo, hi) - lo


def forward_kernel(nf, first, columns, fold, copies, ahead, *refs):
    rows, feats = refs[0], refs[1 : 1 + nf]
    w_ref, cot_ref, cot_ahead_ref = refs[1 + nf : 4 + nf]
    buf, tab, sems = refs[-3:]
    act_ref, delta_ref, *cot_copies = refs[-5 - len(copies) - ahead : -3]
    step, depth, side = w_ref.shape
    per_column = depth // side
    here = pl.program_id(0)

    @pl.when(here == 0)
    def _():
        copy_in([feats], buf, rows, tab, sems)

    index = Index(tab, columns, per_column, fold, side)
    for i in range(step):
        x = index.gather(buf, first + here * step + i, range(per_column))
        lanes = slice(i * side, (i + 1) * side)
        pre, sig, delta = forward_column(x, w_ref[i], cot_ref[:, lanes])
        act_ref[:, lanes] = (pre * sig).astype(BF16)
        delta_ref[:, lanes] = delta
    for ref, (lo, hi) in zip(cot_copies, copies):

        @pl.when((here >= lo) & (here <= hi))
        def _(ref=ref):
            ref[...] = cot_ref[...]

    if ahead:
        cot_copies[-1][...] = cot_ahead_ref[...]


def forward(rows, feats, weight, cotangent, fold, act, first, parts, copied, ahead, step, after=()):
    tokens, hidden = cotangent.shape
    columns, depth, side = weight.shape
    width = sum(f.shape[1] for f in feats)
    count = sum(parts)
    base = first // step
    jump = base + count // step if ahead else base
    args = [rows, *feats, weight, cotangent, cotangent]
    wide = lambda at: pl.BlockSpec((tokens, step * side), lambda i: (0, at + i))
    ins = [ANY] * (1 + len(feats)) + [
        pl.BlockSpec((step, depth, side), lambda i: (base + i, 0, 0)),
        wide(base),
        wide(jump),
    ]
    aliases = {}
    if act is not None:
        aliases = {len(args): 0}
        args.append(act)
    args += after
    ins += [ANY] * (len(args) - len(ins))
    outs = [wide(base), wide(0)]
    spans = ranges(parts, step)
    copies = [spans[n] for n in copied]
    for lo, hi in copies:
        at = held_at(lo, hi)
        outs.append(pl.BlockSpec((tokens, step * side), lambda i, at=at: (0, at(i))))
    sizes = [parts[n] for n in copied]
    if ahead:
        outs.append(wide(0))
        sizes.append(count)
    return pl.pallas_call(
        functools.partial(forward_kernel, len(feats), first, columns, fold, copies, ahead),
        grid=(count // step,),
        in_specs=ins,
        out_specs=outs,
        scratch_shapes=[
            pltpu.VMEM((tokens, width), BF16),
            pltpu.SMEM(rows.shape, jnp.int32),
            pltpu.SemaphoreType.DMA((1 + len(feats),)),
        ],
        out_shape=[
            jax.ShapeDtypeStruct((tokens, hidden), BF16),
            jax.ShapeDtypeStruct((tokens, count * side), BF16),
        ]
        + [jax.ShapeDtypeStruct((tokens, n * side), BF16) for n in sizes],
        input_output_aliases=aliases,
        compiler_params=PARAMS,
        name="forward",
    )(*args)


def block_grads(index, buf, ks, col, delta, scale):
    side = index.side
    x = index.gather(buf, col, ks)
    grad = lax.dot_general(
        x, delta, (((0,), (0,)), ((), ())), preferred_element_type=F32
    )
    return [
        (grad[p * side : (p + 1) * side] * scale).astype(BF16) for p in range(len(ks))
    ]


def grads_kernel(nf, first, columns, fold, scale, *refs):
    rows, mine, other = refs[0], refs[1 : 1 + nf], refs[1 + nf : 1 + 2 * nf]
    w_ref, delta_ref, cot_ref = refs[1 + 2 * nf : 4 + 2 * nf]
    buf, tab, sems = refs[-3:]
    own_ref, rest_ref = refs[-5:-3]
    step, depth, side = w_ref.shape
    per_column = depth // side
    tokens = cot_ref.shape[0]
    here = pl.program_id(0)

    @pl.when(here == 0)
    def _():
        copy_in([mine, other], buf, rows, tab, sems)

    index = Index(tab, columns, per_column, fold, side)
    ks = staged_blocks(1 + rest_ref.shape[0])
    pair = buf.at[pl.ds(tokens, tokens), :]
    done = []
    for i in range(step):
        x = index.gather(pair, first + here * step + i, range(per_column))
        lanes = slice(i * side, (i + 1) * side)
        _, _, delta = forward_column(x, w_ref[i], cot_ref[:, lanes])
        done.append(jnp.concatenate([delta_ref[:, lanes], delta], axis=0))
    for i in range(step):
        blocks = block_grads(index, buf, ks, first + here * step + i, done[i], scale)
        own_ref[i] = blocks[0]
        for p, block in enumerate(blocks[1:]):
            rest_ref[p, i] = block


def grads(
    rows, mine, other, weight, delta, at, cot_other, skip, count, fold, first, line, scale,
    after=(),
):
    tokens = delta.shape[0]
    columns, depth, side = weight.shape
    width = sum(f.shape[1] for f in mine)
    step = math.gcd(first, at, skip, count, STEP)
    base, at, skip = first // step, at // step, skip // step
    args = [rows, *mine, *other, weight, delta, cot_other, *after]
    ins = [ANY] * (1 + 2 * len(mine)) + [
        pl.BlockSpec((step, depth, side), lambda i: (base + i, 0, 0)),
        pl.BlockSpec((tokens, step * side), lambda i: (0, at + i)),
        pl.BlockSpec((tokens, step * side), lambda i: (0, skip + i)),
    ]
    ins += [ANY] * (len(args) - len(ins))
    return pl.pallas_call(
        functools.partial(grads_kernel, len(mine), first, columns, fold, scale),
        grid=(count // step,),
        in_specs=ins,
        out_specs=[
            pl.BlockSpec((step, side, side), lambda i: (i, 0, 0)),
            pl.BlockSpec((line - 1, step, side, side), lambda i: (0, i, 0, 0)),
        ],
        scratch_shapes=[
            pltpu.VMEM((2 * tokens, width), BF16),
            pltpu.SMEM(rows.shape, jnp.int32),
            pltpu.SemaphoreType.DMA((1 + 2 * len(mine),)),
        ],
        out_shape=[
            jax.ShapeDtypeStruct((count, side, side), BF16),
            jax.ShapeDtypeStruct((line - 1, count, side, side), BF16),
        ],
        compiler_params=PARAMS,
        name="grads",
    )(*args)


def dinput_kernel(nd, fold, groups, *refs):
    rows, deltas, w_ref = refs[0], refs[1 : 1 + nd], refs[1 + nd]
    buf, acc, tab, sems = refs[-4:]
    outs = refs[-4 - len(groups) : -4]
    step, depth, side = w_ref.shape
    per_column = depth // side
    here = pl.program_id(0)

    @pl.when(here == 0)
    def _():
        copy_in([deltas], buf, rows, tab, sems)
        acc[...] = jnp.zeros_like(acc)

    index = Index(tab, buf.shape[1] // side, per_column, fold, side)
    for i in range(step):
        col = here * step + i
        d = buf[:, pl.ds(pl.multiple_of(col * side, side), side)]
        g = lax.dot_general(
            d, w_ref[i], (((1,), (1,)), ((), ())), preferred_element_type=F32
        )
        for k in range(per_column):
            acc[index.block(col, k)] += g[:, k * side : (k + 1) * side]

    @pl.when(here == pl.num_programs(0) - 1)
    def _():
        for out, group in zip(outs, groups):
            blocks = out.shape[2] // side
            for n, piece in enumerate(group):
                for b in range(blocks):
                    out[n, :, b * side : (b + 1) * side] = acc[piece * blocks + b].astype(BF16)


def dinput(rows, weight, deltas, fold, groups, width, step, after=()):
    tokens = deltas[0].shape[0]
    columns, depth, side = weight.shape
    pieces = sum(len(g) for g in groups)
    shapes = [(len(g), tokens, width) for g in groups]
    return pl.pallas_call(
        functools.partial(dinput_kernel, len(deltas), fold, groups),
        grid=(columns // step,),
        in_specs=[ANY] * (1 + len(deltas))
        + [pl.BlockSpec((step, depth, side), lambda i: (i, 0, 0))]
        + [ANY] * len(after),
        out_specs=[pl.BlockSpec(s, lambda i: (0, 0, 0)) for s in shapes],
        scratch_shapes=[
            pltpu.VMEM((tokens, columns * side), BF16),
            pltpu.VMEM((pieces * width // side, tokens, side), F32),
            pltpu.SMEM(rows.shape, jnp.int32),
            pltpu.SemaphoreType.DMA((1 + len(deltas),)),
        ],
        out_shape=[jax.ShapeDtypeStruct(s, BF16) for s in shapes],
        compiler_params=PARAMS,
        name="dinput",
    )(rows, *deltas, weight, *after)


def relay_kernel(jobs, *refs):
    outs = refs[-len(jobs) :]
    refs = list(refs)
    for out, parts in zip(outs, jobs):
        at = 0
        for a_at, b_at, count in parts:
            a = refs.pop(0)
            b = None if b_at is None else refs.pop(0)
            wide = a.shape[1]
            for i in range(count):
                value = a[a_at + i]
                if b is not None:
                    value = (value.astype(F32) + b[b_at + i].astype(F32)).astype(BF16)
                out[i, at : at + wide] = value
            at += wide


def relay(*jobs, after=()):
    args, shapes, cuts = [], [], []
    for parts in jobs:
        cuts.append([])
        wide = 0
        for a, a_at, b, b_at, count in parts:
            args += [a] if b is None else [a, b]
            cuts[-1].append((a_at, None if b is None else b_at, count))
            wide += a.shape[1]
        shapes.append((count, wide) + a.shape[2:])
    used = len(args)

    def kernel(*refs):
        relay_kernel(cuts, *refs[:used], *refs[used + len(after) :])

    whole = lambda shape: pl.BlockSpec(shape, lambda i: (0,) * len(shape))
    return pl.pallas_call(
        kernel,
        grid=(1,),
        in_specs=[whole(x.shape) for x in args] + [ANY] * len(after),
        out_specs=[whole(x) for x in shapes],
        out_shape=[jax.ShapeDtypeStruct(x, BF16) for x in shapes],
        compiler_params=PARAMS,
        name="relay",
    )(*args, *after)


def cut_kernel(x_ref, out_ref):
    out_ref[...] = x_ref[...]


def cut(x, width):
    spec = pl.BlockSpec((x.shape[0], width), lambda i: (0, 0))
    return pl.pallas_call(
        cut_kernel,
        grid=(1,),
        in_specs=[spec],
        out_specs=spec,
        out_shape=jax.ShapeDtypeStruct((x.shape[0], width), x.dtype),
        compiler_params=ALL,
        name="cut",
    )(x)


def total_kernel(chunks, *refs):
    out_ref = refs[-1]
    refs = list(refs)
    at = 0
    for count, starts in chunks:
        value = 0.0
        for start in starts:
            ref = refs.pop(0)
            part = ref[0, start : start + count] if len(ref.shape) == 4 else ref[...]
            value = value + part.astype(F32)
        out_ref[at : at + count] = value
        at += count


def total(whole, first, columns, chunks, after=()):
    chunks = [[t if isinstance(t, tuple) else (t, 0) for t in terms] for terms in chunks]
    sizes = [(terms[0][0].shape[0], [start for _, start in terms]) for terms in chunks]
    count = sum(n for n, _ in sizes)
    side = chunks[0][0][0].shape[1]
    base = first // count
    args = [t for terms in chunks for t, _ in terms]
    ins = [
        pl.BlockSpec((1,) + t.shape[1:], lambda i: (0, 0, 0, 0))
        if t.ndim == 4
        else pl.BlockSpec(t.shape, lambda i: (0, 0, 0))
        for t in args
    ]
    used = len(args)
    aliases = {}
    if whole is not None:
        aliases = {len(args): 0}
        args.append(whole)
    args += after

    def kernel(*refs):
        total_kernel(sizes, *refs[:used], refs[-1])

    return pl.pallas_call(
        kernel,
        grid=(1,),
        in_specs=ins + [ANY] * (len(args) - len(ins)),
        out_specs=pl.BlockSpec((count, side, side), lambda i: (base, 0, 0)),
        out_shape=jax.ShapeDtypeStruct((columns, side, side), F32),
        input_output_aliases=aliases,
        compiler_params=PARAMS,
        name="total",
    )(*args)


def gate_kernel(*refs):
    del refs


def gate(x, *after):
    return pl.pallas_call(
        gate_kernel,
        in_specs=[ANY] * (1 + len(after)),
        out_specs=ANY,
        out_shape=jax.ShapeDtypeStruct(x.shape, x.dtype),
        input_output_aliases={0: 0},
        compiler_params=FEW,
        name="gate",
    )(x, *after)


def local_line(features, weight, rows_index, cotangent):
    tokens, held = features.shape
    columns, depth, side = weight.shape
    per_column = depth // side
    replicas, shards = lax.axis_size("replica"), lax.axis_size("shard")
    scale = 1.0 / math.sqrt(tokens * replicas)
    rows = rows_index.reshape(-1)
    fold = held // side
    line = replicas // 2

    def permute(axis, links):
        return lambda x: lax.ppermute(x, axis, links)

    def along(steps):
        return permute("replica", [(a * 2 + p, b * 2 + p) for a, b in steps for p in range(2)])

    cores = permute("shard", [(i, i ^ 1) for i in range(shards)])
    chips = permute("shard", [(i, i ^ 2) for i in range(shards)])
    pairs = permute("replica", [(i, i ^ 1) for i in range(replicas)])
    outer_in = along([(0, 1), (3, 2)])
    middle = along([(1, 2), (2, 1)])
    outer_out = along([(1, 0), (2, 3)])
    beyond = along([(1, 3), (2, 0)])

    sizes = [c * columns // 32 for c in (8, 8, 6, 6, 4)]
    firsts = [sum(sizes[:n]) for n in range(len(sizes))]
    parts = [sizes[0], sizes[1], sizes[2] + sizes[3] + sizes[4]]

    f0 = features
    f2 = chips(f0)
    u0 = pairs(f0)
    cot0 = cut(cotangent, parts[0] * side)
    f2 = gate(f2, cot0, rows)
    c0 = pairs(cot0)
    f1 = cores(f0)
    f3 = cores(f2)
    u1 = cores(u0)
    u2 = chips(u0)
    mine = [f0, f1, f2, f3]
    act, delta0, cot1, cot2 = forward(
        rows, mine, weight, cotangent, fold, None, 0, parts[:2], (1,), True, STEP
    )
    c1, c2 = pairs(cot1), pairs(cot2)
    u2 = gate(u2, delta0, c0)
    u3 = cores(u2)
    other = [u0, u1, u2, u3]

    def chunk(n, delta, cot, *after):
        half = firsts[n] - firsts[2] if n >= 2 else firsts[n]
        return grads(
            rows, mine, other, weight, delta, half, cot, half if n >= 2 else 0, sizes[n], fold,
            firsts[n], line, scale, after,
        )

    own0, rest0 = chunk(0, delta0, c0)
    got0 = outer_in(rest0)
    act, delta1 = forward(
        rows, mine, weight, cotangent, fold, act, firsts[2], parts[2:], (), False, STEP, (own0,)
    )
    own1, rest1 = chunk(1, delta0, c1, delta1)
    got1 = outer_in(rest1)
    near, away0, away1 = dinput(
        rows, weight, [delta0, delta1], fold, ((0, 2), (1,), (3,)), held, STEP, (own1,)
    )
    sib0, sib1 = cores(away0), cores(away1)
    (far0,) = relay([(rest0, 1, got0, 1, 2)], after=(near,))
    across0 = middle(far0)
    own2, rest2 = chunk(2, delta1, c2, far0)
    got2 = outer_in(rest2)
    (far1,) = relay([(rest1, 1, got1, 1, 2)], after=(own2,))
    across1 = middle(far1)
    own3, rest3 = chunk(3, delta1, c2, far1, across0)
    got3 = outer_in(rest3)
    (xsum,) = relay([(near, 1, sib1, 0, 1)], after=(own3, sib0))
    xback = chips(xsum)
    far2, home0 = relay(
        [(rest2, 1, got2, 1, 2)],
        [(rest0, 0, across0, 1, 1), (rest1, 0, across1, 1, 1)],
        after=(xsum,),
    )
    across2 = middle(far2)
    back0 = outer_out(home0)
    own4, rest4 = chunk(4, delta1, c2, far2)
    got4 = outer_in(rest4)
    third0, third1, home1 = relay(
        [(rest3, 1, got3, 1, 1)],
        [(rest3, 2, got3, 2, 1)],
        [(rest2, 0, across2, 1, 1), (rest3, 0, None, 0, 1), (rest4, 0, None, 0, 1)],
        after=(own4, xback),
    )
    near3, far3 = middle(third0), beyond(third1)
    back1 = outer_out(home1)
    last0, last1 = relay(
        [(rest4, 1, got4, 1, 1)], [(rest4, 2, got4, 2, 1)], after=(third0, back0)
    )
    near4, far4 = middle(last0), beyond(last1)
    grad = total(
        None,
        firsts[0],
        columns,
        [[own0, got0, across0, back0], [own1, got1, across1, (back0, sizes[0])]],
        (last0,),
    )
    weight_grad = total(
        grad,
        firsts[2],
        columns,
        [
            [own2, got2, across2, back1],
            [own3, got3, near3, far3, (back1, sizes[2])],
            [own4, got4, near4, far4, (back1, sizes[2] + sizes[3])],
        ],
    )
    input_grad = (
        near[0].astype(F32) + sib0[0].astype(F32) + xback[0].astype(F32)
    ).astype(BF16)
    return act, input_grad, weight_grad


def local_any(features, weight, rows_index, cotangent):
    tokens = features.shape[0]
    columns, depth, side = weight.shape
    per_column = depth // side
    scale = 1.0 / math.sqrt(tokens * lax.axis_size("replica"))
    whole = lax.all_gather(features, "shard", axis=1, tiled=True)
    block_rows = whole.shape[1] // side
    first = lax.axis_index("shard") * columns
    local_rows = lax.dynamic_slice_in_dim(rows_index, first, columns, 0)
    rows = rows_index.reshape(-1)
    step = math.gcd(columns, STEP)
    act, delta = forward(
        rows, [whole], weight, cotangent, 0, None, 0, (columns,), (), False, step
    )
    (part,) = dinput(rows, weight, [delta], 0, ((0,),), whole.shape[1], step)
    input_grad = lax.psum_scatter(part[0], "shard", scatter_dimension=1, tiled=True)
    blocks = whole.reshape(tokens, block_rows, side)[:, local_rows]
    grads = jnp.einsum(
        "qlpf,qlx->lpfx",
        blocks,
        delta.reshape(tokens, columns, side),
        preferred_element_type=F32,
    ).reshape(columns, per_column * side, side)
    weight_grad = lax.psum_scatter(grads, "replica", scatter_dimension=1, tiled=True) * scale
    return act, input_grad, weight_grad


def solution(mesh):
    placed = (P("replica", "shard"), P("shard", None, None), P(), P("replica", "shard"))
    fits = mesh.shape["replica"] == 8 and mesh.shape["shard"] == 4
    return jax.shard_map(
        local_line if fits else local_any,
        mesh=mesh,
        in_specs=placed,
        out_specs=(P("replica", "shard"), P("replica", "shard"), P("shard", "replica", None)),
        check_vma=False,
    )
```

```python
import functools
import math

import jax
import jax.numpy as jnp
from jax import lax
from jax.experimental import pallas as pl
from jax.experimental.pallas import tpu as pltpu
from jax.sharding import PartitionSpec as P

F32 = jnp.float32
BF16 = jnp.bfloat16
ANY = pl.BlockSpec(memory_space=pl.ANY)
PARAMS = pltpu.CompilerParams(
    dimension_semantics=("arbitrary",), vmem_limit_bytes=28 * 1024 * 1024
)
FEW = pltpu.CompilerParams(vmem_limit_bytes=1024 * 1024)
STEP = 4


def copy_in(groups, buf, rows, tab, sems):
    copies = [pltpu.make_async_copy(rows, tab, sems.at[0])]
    top = 0
    for group in groups:
        at = 0
        for ref in group:
            height, width = ref.shape
            copies.append(
                pltpu.make_async_copy(
                    ref,
                    buf.at[pl.ds(top, height), pl.ds(at, width)],
                    sems.at[len(copies)],
                )
            )
            at += width
        top += height
    for copy in copies:
        copy.start()
    for copy in copies:
        copy.wait()


class Index:
    def __init__(self, tab, columns, per_column, fold, side):
        shard = lax.axis_index("shard")
        self.base = shard * columns
        self.flip = shard * fold
        self.tab, self.per_column, self.side = tab, per_column, side

    def block(self, col, k):
        return self.tab[(self.base + col) * self.per_column + k] ^ self.flip

    def lanes(self, col, k):
        return pl.ds(pl.multiple_of(self.block(col, k) * self.side, self.side), self.side)

    def gather(self, buf, col, ks):
        return jnp.concatenate([buf[:, self.lanes(col, k)] for k in ks], axis=1)


def staged_blocks(line):
    r = lax.axis_index("replica")
    z, y = r // 2, r % 2
    inner = (z == 1) | (z == 2)
    one, zero = jnp.int32(1), jnp.int32(0)
    order = [
        jnp.where(inner, one, zero),
        jnp.where(inner, zero, one),
        jnp.int32(2),
        jnp.int32(3),
    ]
    return [jnp.where(z >= line // 2, line - 1 - d, d) * 2 + y for d in order]


def forward_column(x, w, cot):
    pre = jnp.dot(x, w, preferred_element_type=F32)
    sig = 1.0 / (1.0 + jnp.exp(-pre))
    delta = (cot.astype(F32) * sig * (1.0 + pre * (1.0 - sig))).astype(BF16)
    return pre, sig, delta


def ranges(splits, step):
    out, start = [], 0
    for n in splits:
        out.append((start // step, (start + n) // step - 1))
        start += n
    return out


def held_at(lo, hi):
    return lambda i: jnp.clip(i, lo, hi) - lo


def forward_kernel(nf, first, columns, fold, copies, ahead, *refs):
    rows, feats = refs[0], refs[1 : 1 + nf]
    w_ref, cot_ref, cot_ahead_ref = refs[1 + nf : 4 + nf]
    buf, tab, sems = refs[-3:]
    act_ref, delta_ref, *cot_copies = refs[-5 - len(copies) - ahead : -3]
    step, depth, side = w_ref.shape
    per_column = depth // side
    here = pl.program_id(0)

    @pl.when(here == 0)
    def _():
        copy_in([feats], buf, rows, tab, sems)

    index = Index(tab, columns, per_column, fold, side)
    for i in range(step):
        x = index.gather(buf, first + here * step + i, range(per_column))
        lanes = slice(i * side, (i + 1) * side)
        pre, sig, delta = forward_column(x, w_ref[i], cot_ref[:, lanes])
        act_ref[:, lanes] = (pre * sig).astype(BF16)
        delta_ref[:, lanes] = delta
    for ref, (lo, hi) in zip(cot_copies, copies):

        @pl.when((here >= lo) & (here <= hi))
        def _(ref=ref):
            ref[...] = cot_ref[...]

    if ahead:
        cot_copies[-1][...] = cot_ahead_ref[...]


def forward(rows, feats, weight, cotangent, fold, act, first, parts, copied, ahead, step, after=()):
    tokens, hidden = cotangent.shape
    columns, depth, side = weight.shape
    width = sum(f.shape[1] for f in feats)
    count = sum(parts)
    base = first // step
    jump = base + count // step if ahead else base
    args = [rows, *feats, weight, cotangent, cotangent]
    wide = lambda at: pl.BlockSpec((tokens, step * side), lambda i: (0, at + i))
    ins = [ANY] * (1 + len(feats)) + [
        pl.BlockSpec((step, depth, side), lambda i: (base + i, 0, 0)),
        wide(base),
        wide(jump),
    ]
    aliases = {}
    if act is not None:
        aliases = {len(args): 0}
        args.append(act)
    args += after
    ins += [ANY] * (len(args) - len(ins))
    outs = [wide(base), wide(0)]
    spans = ranges(parts, step)
    copies = [spans[n] for n in copied]
    for lo, hi in copies:
        at = held_at(lo, hi)
        outs.append(pl.BlockSpec((tokens, step * side), lambda i, at=at: (0, at(i))))
    sizes = [parts[n] for n in copied]
    if ahead:
        outs.append(wide(0))
        sizes.append(count)
    return pl.pallas_call(
        functools.partial(forward_kernel, len(feats), first, columns, fold, copies, ahead),
        grid=(count // step,),
        in_specs=ins,
        out_specs=outs,
        scratch_shapes=[
            pltpu.VMEM((tokens, width), BF16),
            pltpu.SMEM(rows.shape, jnp.int32),
            pltpu.SemaphoreType.DMA((1 + len(feats),)),
        ],
        out_shape=[
            jax.ShapeDtypeStruct((tokens, hidden), BF16),
            jax.ShapeDtypeStruct((tokens, count * side), BF16),
        ]
        + [jax.ShapeDtypeStruct((tokens, n * side), BF16) for n in sizes],
        input_output_aliases=aliases,
        compiler_params=PARAMS,
        name="forward",
    )(*args)


def block_grads(index, buf, ks, col, delta, scale):
    side = index.side
    x = index.gather(buf, col, ks)
    grad = lax.dot_general(
        x, delta, (((0,), (0,)), ((), ())), preferred_element_type=F32
    )
    return [
        (grad[p * side : (p + 1) * side] * scale).astype(BF16) for p in range(len(ks))
    ]


def grads_kernel(nf, first, columns, fold, scale, *refs):
    rows, mine, other = refs[0], refs[1 : 1 + nf], refs[1 + nf : 1 + 2 * nf]
    w_ref, delta_ref, cot_ref = refs[1 + 2 * nf : 4 + 2 * nf]
    buf, tab, sems = refs[-3:]
    own_ref, rest_ref = refs[-5:-3]
    step, depth, side = w_ref.shape
    per_column = depth // side
    tokens = cot_ref.shape[0]
    here = pl.program_id(0)

    @pl.when(here == 0)
    def _():
        copy_in([mine, other], buf, rows, tab, sems)

    index = Index(tab, columns, per_column, fold, side)
    ks = staged_blocks(1 + rest_ref.shape[0])
    pair = buf.at[pl.ds(tokens, tokens), :]
    done = []
    for i in range(step):
        x = index.gather(pair, first + here * step + i, range(per_column))
        lanes = slice(i * side, (i + 1) * side)
        _, _, delta = forward_column(x, w_ref[i], cot_ref[:, lanes])
        done.append(jnp.concatenate([delta_ref[:, lanes], delta], axis=0))
    for i in range(step):
        blocks = block_grads(index, buf, ks, first + here * step + i, done[i], scale)
        own_ref[i] = blocks[0]
        for p, block in enumerate(blocks[1:]):
            rest_ref[p, i] = block


def grads(
    rows, mine, other, weight, delta, at, cot_other, skip, count, fold, first, line, scale,
    after=(),
):
    tokens = delta.shape[0]
    columns, depth, side = weight.shape
    width = sum(f.shape[1] for f in mine)
    step = math.gcd(first, at, skip, count, STEP)
    base, at, skip = first // step, at // step, skip // step
    args = [rows, *mine, *other, weight, delta, cot_other, *after]
    ins = [ANY] * (1 + 2 * len(mine)) + [
        pl.BlockSpec((step, depth, side), lambda i: (base + i, 0, 0)),
        pl.BlockSpec((tokens, step * side), lambda i: (0, at + i)),
        pl.BlockSpec((tokens, step * side), lambda i: (0, skip + i)),
    ]
    ins += [ANY] * (len(args) - len(ins))
    return pl.pallas_call(
        functools.partial(grads_kernel, len(mine), first, columns, fold, scale),
        grid=(count // step,),
        in_specs=ins,
        out_specs=[
            pl.BlockSpec((step, side, side), lambda i: (i, 0, 0)),
            pl.BlockSpec((line - 1, step, side, side), lambda i: (0, i, 0, 0)),
        ],
        scratch_shapes=[
            pltpu.VMEM((2 * tokens, width), BF16),
            pltpu.SMEM(rows.shape, jnp.int32),
            pltpu.SemaphoreType.DMA((1 + 2 * len(mine),)),
        ],
        out_shape=[
            jax.ShapeDtypeStruct((count, side, side), BF16),
            jax.ShapeDtypeStruct((line - 1, count, side, side), BF16),
        ],
        compiler_params=PARAMS,
        name="grads",
    )(*args)


def dinput_kernel(nd, fold, groups, *refs):
    rows, deltas, w_ref = refs[0], refs[1 : 1 + nd], refs[1 + nd]
    buf, acc, tab, sems = refs[-4:]
    outs = refs[-4 - len(groups) : -4]
    step, depth, side = w_ref.shape
    per_column = depth // side
    here = pl.program_id(0)

    @pl.when(here == 0)
    def _():
        copy_in([deltas], buf, rows, tab, sems)
        acc[...] = jnp.zeros_like(acc)

    index = Index(tab, buf.shape[1] // side, per_column, fold, side)
    for i in range(step):
        col = here * step + i
        d = buf[:, pl.ds(pl.multiple_of(col * side, side), side)]
        g = lax.dot_general(
            d, w_ref[i], (((1,), (1,)), ((), ())), preferred_element_type=F32
        )
        for k in range(per_column):
            acc[index.block(col, k)] += g[:, k * side : (k + 1) * side]

    @pl.when(here == pl.num_programs(0) - 1)
    def _():
        for out, group in zip(outs, groups):
            blocks = out.shape[2] // side
            for n, piece in enumerate(group):
                for b in range(blocks):
                    out[n, :, b * side : (b + 1) * side] = acc[piece * blocks + b].astype(BF16)


def dinput(rows, weight, deltas, fold, groups, width, step, after=()):
    tokens = deltas[0].shape[0]
    columns, depth, side = weight.shape
    pieces = sum(len(g) for g in groups)
    shapes = [(len(g), tokens, width) for g in groups]
    return pl.pallas_call(
        functools.partial(dinput_kernel, len(deltas), fold, groups),
        grid=(columns // step,),
        in_specs=[ANY] * (1 + len(deltas))
        + [pl.BlockSpec((step, depth, side), lambda i: (i, 0, 0))]
        + [ANY] * len(after),
        out_specs=[pl.BlockSpec(s, lambda i: (0, 0, 0)) for s in shapes],
        scratch_shapes=[
            pltpu.VMEM((tokens, columns * side), BF16),
            pltpu.VMEM((pieces * width // side, tokens, side), F32),
            pltpu.SMEM(rows.shape, jnp.int32),
            pltpu.SemaphoreType.DMA((1 + len(deltas),)),
        ],
        out_shape=[jax.ShapeDtypeStruct(s, BF16) for s in shapes],
        compiler_params=PARAMS,
        name="dinput",
    )(rows, *deltas, weight, *after)


def relay_kernel(jobs, *refs):
    outs = refs[-len(jobs) :]
    refs = list(refs)
    for out, parts in zip(outs, jobs):
        at = 0
        for a_at, b_at, count in parts:
            a = refs.pop(0)
            b = None if b_at is None else refs.pop(0)
            wide = a.shape[1]
            for i in range(count):
                value = a[a_at + i]
                if b is not None:
                    value = (value.astype(F32) + b[b_at + i].astype(F32)).astype(BF16)
                out[i, at : at + wide] = value
            at += wide


def relay(*jobs, after=()):
    args, shapes, cuts = [], [], []
    for parts in jobs:
        cuts.append([])
        wide = 0
        for a, a_at, b, b_at, count in parts:
            args += [a] if b is None else [a, b]
            cuts[-1].append((a_at, None if b is None else b_at, count))
            wide += a.shape[1]
        shapes.append((count, wide) + a.shape[2:])
    used = len(args)

    def kernel(*refs):
        relay_kernel(cuts, *refs[:used], *refs[used + len(after) :])

    whole = lambda shape: pl.BlockSpec(shape, lambda i: (0,) * len(shape))
    return pl.pallas_call(
        kernel,
        grid=(1,),
        in_specs=[whole(x.shape) for x in args] + [ANY] * len(after),
        out_specs=[whole(x) for x in shapes],
        out_shape=[jax.ShapeDtypeStruct(x, BF16) for x in shapes],
        compiler_params=PARAMS,
        name="relay",
    )(*args, *after)


def cut_kernel(x_ref, out_ref):
    out_ref[...] = x_ref[...]


def cut(x, width):
    spec = pl.BlockSpec((x.shape[0], width), lambda i: (0, 0))
    return pl.pallas_call(
        cut_kernel,
        grid=(1,),
        in_specs=[spec],
        out_specs=spec,
        out_shape=jax.ShapeDtypeStruct((x.shape[0], width), x.dtype),
        compiler_params=PARAMS,
        name="cut",
    )(x)


def total_kernel(chunks, *refs):
    out_ref = refs[-1]
    refs = list(refs)
    at = 0
    for count, starts in chunks:
        value = 0.0
        for start in starts:
            ref = refs.pop(0)
            part = ref[0, start : start + count] if len(ref.shape) == 4 else ref[...]
            value = value + part.astype(F32)
        out_ref[at : at + count] = value
        at += count


def total(whole, first, columns, chunks, after=()):
    chunks = [[t if isinstance(t, tuple) else (t, 0) for t in terms] for terms in chunks]
    sizes = [(terms[0][0].shape[0], [start for _, start in terms]) for terms in chunks]
    count = sum(n for n, _ in sizes)
    side = chunks[0][0][0].shape[1]
    base = first // count
    args = [t for terms in chunks for t, _ in terms]
    ins = [
        pl.BlockSpec((1,) + t.shape[1:], lambda i: (0, 0, 0, 0))
        if t.ndim == 4
        else pl.BlockSpec(t.shape, lambda i: (0, 0, 0))
        for t in args
    ]
    used = len(args)
    aliases = {}
    if whole is not None:
        aliases = {len(args): 0}
        args.append(whole)
    args += after

    def kernel(*refs):
        total_kernel(sizes, *refs[:used], refs[-1])

    return pl.pallas_call(
        kernel,
        grid=(1,),
        in_specs=ins + [ANY] * (len(args) - len(ins)),
        out_specs=pl.BlockSpec((count, side, side), lambda i: (base, 0, 0)),
        out_shape=jax.ShapeDtypeStruct((columns, side, side), F32),
        input_output_aliases=aliases,
        compiler_params=PARAMS,
        name="total",
    )(*args)


def gate_kernel(*refs):
    del refs


def gate(x, *after):
    return pl.pallas_call(
        gate_kernel,
        in_specs=[ANY] * (1 + len(after)),
        out_specs=ANY,
        out_shape=jax.ShapeDtypeStruct(x.shape, x.dtype),
        input_output_aliases={0: 0},
        compiler_params=FEW,
        name="gate",
    )(x, *after)


def local_line(features, weight, rows_index, cotangent):
    tokens, held = features.shape
    columns, depth, side = weight.shape
    per_column = depth // side
    replicas, shards = lax.axis_size("replica"), lax.axis_size("shard")
    scale = 1.0 / math.sqrt(tokens * replicas)
    rows = rows_index.reshape(-1)
    fold = held // side
    line = replicas // 2

    def permute(axis, links):
        return lambda x: lax.ppermute(x, axis, links)

    def along(steps):
        return permute("replica", [(a * 2 + p, b * 2 + p) for a, b in steps for p in range(2)])

    cores = permute("shard", [(i, i ^ 1) for i in range(shards)])
    chips = permute("shard", [(i, i ^ 2) for i in range(shards)])
    pairs = permute("replica", [(i, i ^ 1) for i in range(replicas)])
    outer_in = along([(0, 1), (3, 2)])
    middle = along([(1, 2), (2, 1)])
    outer_out = along([(1, 0), (2, 3)])
    beyond = along([(1, 3), (2, 0)])

    sizes = [c * columns // 32 for c in (8, 8, 6, 6, 4)]
    firsts = [sum(sizes[:n]) for n in range(len(sizes))]
    parts = [sizes[0], sizes[1], sizes[2] + sizes[3] + sizes[4]]

    f0 = features
    f2 = chips(f0)
    u0 = pairs(f0)
    cot0 = cut(cotangent, parts[0] * side)
    f2 = gate(f2, cot0, rows)
    c0 = pairs(cot0)
    f1 = cores(f0)
    f3 = cores(f2)
    u1 = cores(u0)
    u2 = chips(u0)
    mine = [f0, f1, f2, f3]
    act, delta0, cot1, cot2 = forward(
        rows, mine, weight, cotangent, fold, None, 0, parts[:2], (1,), True, STEP
    )
    c1, c2 = pairs(cot1), pairs(cot2)
    u2 = gate(u2, delta0, c0)
    u3 = cores(u2)
    other = [u0, u1, u2, u3]

    def chunk(n, delta, cot, *after):
        half = firsts[n] - firsts[2] if n >= 2 else firsts[n]
        return grads(
            rows, mine, other, weight, delta, half, cot, half if n >= 2 else 0, sizes[n], fold,
            firsts[n], line, scale, after,
        )

    own0, rest0 = chunk(0, delta0, c0)
    got0 = outer_in(rest0)
    act, delta1 = forward(
        rows, mine, weight, cotangent, fold, act, firsts[2], parts[2:], (), False, STEP, (own0,)
    )
    own1, rest1 = chunk(1, delta0, c1, delta1)
    got1 = outer_in(rest1)
    near, away0, away1 = dinput(
        rows, weight, [delta0, delta1], fold, ((0, 2), (1,), (3,)), held, STEP, (own1,)
    )
    sib0, sib1 = cores(away0), cores(away1)
    (far0,) = relay([(rest0, 1, got0, 1, 2)], after=(near,))
    across0 = middle(far0)
    own2, rest2 = chunk(2, delta1, c2, far0)
    got2 = outer_in(rest2)
    (far1,) = relay([(rest1, 1, got1, 1, 2)], after=(own2,))
    across1 = middle(far1)
    own3, rest3 = chunk(3, delta1, c2, far1, across0)
    got3 = outer_in(rest3)
    (xsum,) = relay([(near, 1, sib1, 0, 1)], after=(own3, sib0))
    xback = chips(xsum)
    far2, home0 = relay(
        [(rest2, 1, got2, 1, 2)],
        [(rest0, 0, across0, 1, 1), (rest1, 0, across1, 1, 1)],
        after=(xsum,),
    )
    across2 = middle(far2)
    back0 = outer_out(home0)
    own4, rest4 = chunk(4, delta1, c2, far2)
    got4 = outer_in(rest4)
    third0, third1, home1 = relay(
        [(rest3, 1, got3, 1, 1)],
        [(rest3, 2, got3, 2, 1)],
        [(rest2, 0, across2, 1, 1), (rest3, 0, None, 0, 1), (rest4, 0, None, 0, 1)],
        after=(own4, xback),
    )
    near3, far3 = middle(third0), beyond(third1)
    back1 = outer_out(home1)
    last0, last1 = relay(
        [(rest4, 1, got4, 1, 1)], [(rest4, 2, got4, 2, 1)], after=(third0, back0)
    )
    near4, far4 = middle(last0), beyond(last1)
    grad = total(
        None,
        firsts[0],
        columns,
        [[own0, got0, across0, back0], [own1, got1, across1, (back0, sizes[0])]],
        (last0,),
    )
    weight_grad = total(
        grad,
        firsts[2],
        columns,
        [
            [own2, got2, across2, back1],
            [own3, got3, near3, far3, (back1, sizes[2])],
            [own4, got4, near4, far4, (back1, sizes[2] + sizes[3])],
        ],
    )
    input_grad = (
        near[0].astype(F32) + sib0[0].astype(F32) + xback[0].astype(F32)
    ).astype(BF16)
    return act, input_grad, weight_grad


def local_any(features, weight, rows_index, cotangent):
    tokens = features.shape[0]
    columns, depth, side = weight.shape
    per_column = depth // side
    scale = 1.0 / math.sqrt(tokens * lax.axis_size("replica"))
    whole = lax.all_gather(features, "shard", axis=1, tiled=True)
    block_rows = whole.shape[1] // side
    first = lax.axis_index("shard") * columns
    local_rows = lax.dynamic_slice_in_dim(rows_index, first, columns, 0)
    rows = rows_index.reshape(-1)
    step = math.gcd(columns, STEP)
    act, delta = forward(
        rows, [whole], weight, cotangent, 0, None, 0, (columns,), (), False, step
    )
    (part,) = dinput(rows, weight, [delta], 0, ((0,),), whole.shape[1], step)
    input_grad = lax.psum_scatter(part[0], "shard", scatter_dimension=1, tiled=True)
    blocks = whole.reshape(tokens, block_rows, side)[:, local_rows]
    grads = jnp.einsum(
        "qlpf,qlx->lpfx",
        blocks,
        delta.reshape(tokens, columns, side),
        preferred_element_type=F32,
    ).reshape(columns, per_column * side, side)
    weight_grad = lax.psum_scatter(grads, "replica", scatter_dimension=1, tiled=True) * scale
    return act, input_grad, weight_grad


def solution(mesh):
    placed = (P("replica", "shard"), P("shard", None, None), P(), P("replica", "shard"))
    fits = mesh.shape["replica"] == 8 and mesh.shape["shard"] == 4
    return jax.shard_map(
        local_line if fits else local_any,
        mesh=mesh,
        in_specs=placed,
        out_specs=(P("replica", "shard"), P("replica", "shard"), P("shard", "replica", None)),
        check_vma=False,
    )
```
